128 devices in a mesh: grp: 8 (over z, core), mem: 16 (over y, x).
Axes of the slice: x: 4, y: 4, z: 4, core: 2. Of those that a mesh axis runs over, the one named last changes fastest.
Arguments:
- a_tiles: bfloat16 [6144, 7, 128, 128], P(('grp', 'mem')), may hold values from -0.1875 to 0.1875
- p_tiles: bfloat16 [6144, 3, 128, 128], P(('grp', 'mem')), may hold values from -0.5 to 0.5
- a_offsets: int32 [6144, 7], P(('grp', 'mem')), may hold values from -4 to 4, as said below
- agg_counts: int32 [8, 16], replicated, may hold values from 1 to 12, as said below
- row_counts: int32 [8, 16], replicated, may hold values from 4 to 48, as said below
- flows: int32 [8, 2], replicated, may hold values from 1 to 12, as said below
Outputs:
- coarse_tiles: float32 [944, 7, 128, 128], P('grp', None, 'mem')
The draws below stay inside these ranges and needn't reach their ends.
Inputs may be any that keep to these rules, and one draw needn't show every extreme that they name: `a_offsets`: each row's 7 offsets are distinct, the first is 0 and the others are nonzero. `agg_counts`: the counts of the 16 devices of each group sum to 96; in every group some device has 12 and some has 1. `row_counts`: each device has between 4 and 8 times its aggregate count of live rows, and at most 48; a device with 12 aggregates has 48 rows. `flows`: both ends are reached in every draw, and some group owns 118 coarse rows.
All inputs are finite; a program needn't handle non-finite values.
Results may differ from the reference program's by a relative error of at most 0.0029.
Values may be sent and summed in bfloat16 or wider, within the bound.
A program may use at most 128 MiB of HBM per device.

```python
import jax
import jax.numpy as jnp
from jax import lax

TILE = 128
A_TILES = 7
P_TILES = 3
RCAP = 48
BAND = 7
GMAX = 12
GROUP_ROWS = 96
FMAX = 12
OCAP = 118
SLOTS = 6144
N_GRP = 8
N_MEM = 16


def counts_table(key):
    half_cap = GMAX // 2
    key_pairs, key_second, key_order = jax.random.split(key, 3)
    shifts = jax.random.randint(key_pairs, (N_GRP, N_MEM // 2), -(half_cap - 1), half_cap)
    pairs = jnp.stack([half_cap + shifts, half_cap - shifts], -1)
    second = jax.random.randint(key_second, (N_GRP,), -(half_cap - 2), half_cap - 1)
    pairs = pairs.at[:, 0, 0].set(GMAX)
    pairs = pairs.at[:, 0, 1].set(1)
    pairs = pairs.at[:, 1, 0].set(half_cap + second)
    pairs = pairs.at[:, 1, 1].set(half_cap - 1 - second)
    values = pairs.reshape(N_GRP, N_MEM)
    order_keys = jax.random.split(key_order, N_GRP)
    orders = jax.vmap(lambda single: jax.random.permutation(single, N_MEM))(order_keys)
    return jnp.take_along_axis(values, orders, axis=1).astype(jnp.int32)


def draw_agg_counts(key, part):
    shared = counts_table(key)
    return shared


def draw_row_counts(key, part):
    shared = counts_table(key)
    key = jax.random.fold_in(key, 12)
    extra = jax.random.randint(key, shared.shape, 0, 4 * shared + 1)
    return jnp.minimum(4 * shared + extra, RCAP).astype(jnp.int32)


def draw_a_offsets(key, part):
    key = jax.random.fold_in(key, 13)
    candidates = jnp.array([-4, -3, -2, -1, 1, 2, 3, 4], jnp.int32)
    row_keys = jax.random.split(key, SLOTS)
    chosen = jax.vmap(lambda single: jax.random.permutation(single, candidates))(row_keys)[:, :A_TILES - 1]
    return jnp.concatenate([jnp.zeros((SLOTS, 1), jnp.int32), chosen], 1).astype(jnp.int32)


def draw_flows(key, part):
    key = jax.random.fold_in(key, 14)
    key_values, key_turn = jax.random.split(key)
    values = jax.random.randint(key_values, (N_GRP, 2), 1, FMAX + 1)
    values = values.at[0, 0].set(FMAX)
    values = values.at[2, 1].set(FMAX)
    values = values.at[1, 0].set(1)
    values = values.at[1, 1].set(1)
    turn = jax.random.randint(key_turn, (), 0, N_GRP)
    return jnp.roll(values, turn, axis=0).astype(jnp.int32)


def levels(rng, dims, pieces, low, largest):
    loudness, own = 1.0, jax.random.fold_in(rng, 6)
    for position, blocks in pieces:
        draws = jnp.exp(jax.random.uniform(jax.random.fold_in(own, position), (blocks,), jnp.float32, low / len(pieces), largest / len(pieces)))
        loudness = loudness * jnp.repeat(draws, dims[position] // blocks).reshape([-1 if axis == position else 1 for axis in range(len(dims))])
    return loudness


def noise(rng, extent, scale, most, cuts=(), kind=jnp.bfloat16):
    level = levels(rng, extent, cuts, -0.22, 0.18) if cuts else 1.0
    entries = jax.random.normal(rng, extent, jnp.float32) * scale * level
    return jnp.minimum(jnp.maximum(entries, -most), most).astype(kind)


def setup_inputs(seed: int = 0) -> dict:
    arg_keys = jax.random.split(jax.random.key(seed), 7)
    return {
        "a_tiles": noise(arg_keys[0], (SLOTS, A_TILES, TILE, TILE), (A_TILES * TILE) ** -0.5, 0.1875, ((0, 128),)),
        "p_tiles": noise(arg_keys[1], (SLOTS, P_TILES, TILE, TILE), TILE ** -0.5, 0.5, ((0, 128),)),
        "a_offsets": draw_a_offsets(jax.random.fold_in(arg_keys[6], 71), 0),
        "agg_counts": draw_agg_counts(jax.random.fold_in(arg_keys[6], 71), 0),
        "row_counts": draw_row_counts(jax.random.fold_in(arg_keys[6], 71), 0),
        "flows": draw_flows(jax.random.fold_in(arg_keys[6], 71), 0),
    }


def device_part(index, a_blocks, p_blocks, offsets, flat_aggs, flat_rows):
    devices = N_GRP * N_MEM
    before = (index - 1) % devices
    after_dev = (index + 1) % devices
    own_rows = flat_rows[index]
    own_aggs = flat_aggs[index]
    prev_rows = flat_rows[before]
    ghost_table = jnp.concatenate([p_blocks[before], p_blocks[index], p_blocks[after_dev]], 0)
    row_ids = jnp.arange(RCAP, dtype=jnp.int32)
    row_agg = (row_ids * own_aggs) // own_rows
    target = row_ids[:, None] + offsets[index]
    table_row = jnp.where(target < 0, prev_rows + target,
                          jnp.where(target < own_rows, RCAP + target, 2 * RCAP + target - own_rows))
    table_row = jnp.clip(table_row, 0, 3 * RCAP - 1).astype(jnp.int32)
    their_agg = jnp.where(target < 0, -1, jnp.where(target < own_rows, (target * own_aggs) // own_rows, own_aggs))
    live_mask = row_ids < own_rows
    band_slot = (their_agg - row_agg[:, None])[:, :, None] + jnp.arange(3, dtype=jnp.int32)[None, None, :] + 1
    band_slot = jnp.clip(band_slot, 0, 4).astype(jnp.int32)
    gathered = ghost_table[table_row]
    products = jnp.einsum("rkab,rkqbc->rkqac", a_blocks[index].astype(jnp.float32), gathered.astype(jnp.float32))
    products = products * live_mask[:, None, None, None, None]
    line_ids = jnp.broadcast_to(row_ids[:, None, None], band_slot.shape)
    merged = jnp.zeros((RCAP, 5, TILE, TILE), jnp.float32).at[line_ids, band_slot].add(products)
    merged = merged.astype(jnp.bfloat16)
    triple = jnp.einsum("rpba,rebc->rpeac", p_blocks[index].astype(jnp.float32), merged.astype(jnp.float32))
    triple = triple * live_mask[:, None, None, None, None]
    slot_ids = row_agg[:, None, None] + jnp.arange(3, dtype=jnp.int32)[None, :, None] + jnp.zeros((1, 1, 5), jnp.int32)
    slot_ids = jnp.clip(slot_ids, 0, GMAX + 1).astype(jnp.int32)
    column_ids = jnp.arange(5, dtype=jnp.int32)[None, None, :] - jnp.arange(3, dtype=jnp.int32)[None, :, None] + 2
    column_ids = jnp.broadcast_to(column_ids, slot_ids.shape).astype(jnp.int32)
    return jnp.zeros((GMAX + 2, BAND, TILE, TILE), jnp.float32).at[slot_ids, column_ids].add(triple)


def reference(a_tiles, p_tiles, a_offsets, agg_counts, row_counts, flows):
    devices = N_GRP * N_MEM
    a_blocks = a_tiles.reshape(devices, RCAP, A_TILES, TILE, TILE)
    p_blocks = p_tiles.reshape(devices, RCAP, P_TILES, TILE, TILE)
    offsets = a_offsets.reshape(devices, RCAP, A_TILES)
    flat_aggs = agg_counts.reshape(-1)
    flat_rows = row_counts.reshape(-1)
    parts = lax.map(lambda index: device_part(index, a_blocks, p_blocks, offsets, flat_aggs, flat_rows),
                    jnp.arange(devices, dtype=jnp.int32))
    first_slot = parts[:, 0]
    last_slot = parts[jnp.arange(devices, dtype=jnp.int32), flat_aggs + 1]
    from_after = jnp.roll(first_slot, -1, axis=0)
    from_before = jnp.roll(last_slot, 1, axis=0)
    local_ids = jnp.arange(GMAX, dtype=jnp.int32)[None, :]
    complete = parts[:, 1:GMAX + 1]
    complete = complete + (local_ids == flat_aggs[:, None] - 1)[:, :, None, None, None] * from_after[:, None]
    complete = complete + (local_ids == 0)[:, :, None, None, None] * from_before[:, None]
    live_rows = local_ids < flat_aggs[:, None]
    complete = complete * live_rows[:, :, None, None, None]
    total_rows = N_GRP * GROUP_ROWS
    begins = jnp.cumsum(flat_aggs) - flat_aggs
    global_ids = jnp.where(live_rows, begins[:, None] + local_ids, total_rows).astype(jnp.int32)
    coarse = jnp.zeros((total_rows, BAND, TILE, TILE), jnp.float32)
    coarse = coarse.at[global_ids.reshape(-1)].add(complete.reshape(-1, BAND, TILE, TILE), mode="drop")
    group_ids = jnp.arange(N_GRP, dtype=jnp.int32)
    forward = flows[:, 0]
    backward = flows[:, 1]
    take_lower = forward[(group_ids - 1) % N_GRP][:, None]
    take_upper = backward[(group_ids + 1) % N_GRP][:, None]
    middle = (GROUP_ROWS - forward - backward)[:, None]
    base = (group_ids * GROUP_ROWS)[:, None]
    slot_ids = jnp.arange(OCAP, dtype=jnp.int32)[None, :]
    global_row = jnp.where(slot_ids < take_lower, base - take_lower + slot_ids,
                           jnp.where(slot_ids < take_lower + middle,
                                     base + backward[:, None] + slot_ids - take_lower,
                                     base + GROUP_ROWS + slot_ids - take_lower - middle))
    taken = (global_row % total_rows).astype(jnp.int32)
    keep = slot_ids < take_lower + middle + take_upper
    result = coarse[taken] * keep[:, :, None, None, None]
    return result.reshape(N_GRP * OCAP, BAND, TILE, TILE)
```

```python
import functools

import jax
import jax.numpy as jnp
from jax import lax
from jax.experimental import pallas as pl
from jax.experimental.pallas import tpu as pltpu
from jax.sharding import PartitionSpec as P

MESH = pl.DeviceIdType.MESH
F32 = jnp.float32
BF16 = jnp.bfloat16
KA = 7
KP = 3
BAND = 7
HALO = 4
WIDE = 5
CHUNK = 4
LONG = 8


def fused(sizes, a_hbm, p_hbm, offs, aggs, rows, flows, out_hbm,
          a_all, own, edge, ghost_out, ap, pt, band, near, send, recv, wide, outv, zsend, zrecv,
          start_tab, agg_tab, row_tab,
          a_sem, p_sem, halo_send, halo_recv, send_sem, recv_sem, self_sem, z_send, z_recv, out_sem):
    groups, members, cap, tile = sizes
    gmax = cap // 4
    pairs = gmax // 2
    coarse = members * gmax // 2
    fmax = coarse // 8
    out_cap = outv.shape[0]
    share = tile // members
    slots = gmax + 2
    spill = pairs * BAND
    total = spill + WIDE
    inner = cap - 2 * HALO
    grp = lax.axis_index("grp")
    mem = lax.axis_index("mem")
    up, down = lax.rem(grp + 1, groups), lax.rem(grp + groups - 1, groups)
    last = (mem == members - 1).astype(jnp.int32)
    first = (mem == 0).astype(jnp.int32)
    next_dev = (lax.rem(grp + last, groups), lax.rem(mem + 1, members))
    prev_dev = (lax.rem(grp + groups - first, groups), lax.rem(mem + members - 1, members))

    def p_copy(r):
        return pltpu.make_async_copy(p_hbm.at[r], own.at[pl.ds(WIDE * r + 2, KP)], p_sem)

    def a_copy(c):
        return pltpu.make_async_copy(
            a_hbm.at[pl.ds(c * CHUNK, CHUNK)], a_all.at[pl.ds(c * CHUNK, CHUNK)], a_sem.at[c])

    lax.fori_loop(0, cap, lambda r, _: (p_copy(r).start(), 0)[1], 0)
    lax.fori_loop(0, cap // CHUNK, lambda c, _: (a_copy(c).start(), 0)[1], 0)

    barrier = pltpu.get_barrier_semaphore()

    def greet(step, _):
        pl.semaphore_signal(barrier, inc=1, device_id=(grp, lax.rem(mem + step, members)), device_id_type=MESH)
        return 0

    lax.fori_loop(1, members, greet, 0)
    for device in ((up, mem), (down, mem), next_dev, prev_dev):
        pl.semaphore_signal(barrier, inc=1, device_id=device, device_id_type=MESH)

    n = rows[grp, mem]
    ga = aggs[grp, mem]

    def fill_agg(r, carry):
        agg, rest = carry
        agg_tab[r] = agg
        rest = rest + ga
        step = (rest >= n).astype(jnp.int32)
        return jnp.minimum(agg + step, gmax), rest - step * n

    lax.fori_loop(0, cap, fill_agg, (jnp.int32(0), jnp.int32(0)))

    def fill_start(a, carry):
        q, rest = carry
        start_tab[a] = jnp.minimum(q + (rest > 0).astype(jnp.int32), n)
        rest = rest + n
        for _ in range(LONG):
            step = (rest >= ga).astype(jnp.int32)
            q, rest = q + step, rest - step * ga
        return q, rest

    lax.fori_loop(0, gmax + 2, fill_start, (jnp.int32(0), jnp.int32(0)))

    def fill_row(c, carry):
        who, place = carry
        count = aggs[grp, who]
        slot = jnp.where(place < 2, gmax - 4 + place,
                         jnp.where(place >= count - 2, gmax + place - count, gmax - 2 + place - count))
        row_tab[c] = who * slots + jnp.clip(slot, 0, gmax - 1)
        done = (place + 1 >= count).astype(jnp.int32)
        return jnp.minimum(who + done, members - 1), (1 - done) * (place + 1)

    lax.fori_loop(0, coarse, fill_row, (jnp.int32(0), jnp.int32(0)))

    blank = jnp.zeros((tile, tile), BF16)

    def blank_row(table):
        def body(r, _):
            table[WIDE * r] = blank
            table[WIDE * r + 1] = blank
            return 0
        return body

    lax.fori_loop(0, cap + 1, blank_row(own), 0)
    lax.fori_loop(0, 6 * HALO + 1, blank_row(edge), 0)
    pt[cap] = jnp.zeros((KP * tile, tile), BF16)

    def blank_band(s, _):
        band[s] = jnp.zeros((BAND, tile, tile), F32)
        return 0

    lax.fori_loop(0, gmax + 2, blank_band, 0)

    whole = own.at[pl.ds(0, KP * cap)]
    pltpu.make_async_copy(whole, whole, p_sem).wait()
    for r in range(HALO):
        for q in range(KP):
            ghost_out[KP * r + q] = own[WIDE * jnp.maximum(n - HALO + r, 0) + 2 + q]
    pl.semaphore_wait(barrier, members - 1 + 4)

    def to_next(r):
        return pltpu.make_async_remote_copy(
            src_ref=ghost_out.at[pl.ds(KP * r, KP)], dst_ref=edge.at[pl.ds(WIDE * r + 2, KP)],
            send_sem=halo_send.at[r], recv_sem=halo_recv.at[r], device_id=next_dev, device_id_type=MESH)

    def to_prev(r):
        return pltpu.make_async_remote_copy(
            src_ref=own.at[pl.ds(WIDE * r + 2, KP)], dst_ref=edge.at[pl.ds(WIDE * (5 * HALO + r) + 2, KP)],
            send_sem=halo_send.at[HALO + r], recv_sem=halo_recv.at[HALO + r],
            device_id=prev_dev, device_id_type=MESH)

    for r in range(HALO):
        to_next(r).start()
        to_prev(r).start()

    for r in range(2 * HALO):
        for q in range(KP):
            edge[WIDE * (HALO + r) + 2 + q] = own[WIDE * r + 2 + q]
            edge[WIDE * (3 * HALO + r) + 2 + q] = own[WIDE * jnp.maximum(n - 2 * HALO + r, 0) + 2 + q]

    def ap_row(position, row, table, index_of):
        agg = agg_tab[row]
        begin, end = start_tab[agg], start_tab[agg + 1]
        bases = []
        for k in range(KA):
            target = row + offs[k, row]
            delta = (target >= end).astype(jnp.int32) - (target < begin).astype(jnp.int32)
            bases.append(WIDE * index_of(target) + 1 - delta)
        lhs = jnp.concatenate([a_all[row, k] for k in range(KA)], axis=1)
        for low, high in ((0, 2), (2, 4), (4, 5)):
            rhs = jnp.concatenate(
                [jnp.concatenate([table[b + e] for e in range(low, high)], axis=1) for b in bases], axis=0)
            out = jnp.dot(lhs, rhs, preferred_element_type=F32).astype(BF16)
            for e in range(low, high):
                ap[position, e] = out[:, (e - low) * tile:(e - low + 1) * tile]
        for q in range(KP):
            pt[position, pl.ds(q * tile, tile), :] = own[WIDE * row + 2 + q].T

    def inner_index(target):
        return jnp.clip(target, 0, cap - 1)

    def edge_index(target):
        from_end = 5 * HALO + target - n
        index = jnp.where(jnp.logical_or(target >= n, target >= 2 * HALO), from_end, HALO + target)
        return jnp.clip(index, 0, 6 * HALO - 1)

    def place_of(row):
        place = jnp.where(row < HALO, inner + row, jnp.where(row >= n - HALO, cap - n + row, row - HALO))
        return jnp.clip(place, 0, cap - 1)

    def products(begin, end, put):
        left, right = [], []
        for t in range(LONG):
            live = begin + t < end
            place = place_of(begin + t)
            left.append(jnp.where(live, place, cap))
            right.append(jnp.where(live, place, 0))
        lhs = jnp.concatenate([pt[i] for i in left], axis=1)
        for low, high in ((0, 2), (2, 4), (4, 5)):
            rhs = jnp.concatenate(
                [jnp.concatenate([ap[i, e] for e in range(low, high)], axis=1) for i in right], axis=0)
            out = jnp.dot(lhs, rhs, preferred_element_type=F32)
            for e in range(low, high):
                for q in range(KP):
                    put(q, e, out[q * tile:(q + 1) * tile, (e - low) * tile:(e - low + 1) * tile])

    def aggregate(back):
        agg = back + ga - gmax
        begin = start_tab[jnp.maximum(agg, 0)]
        end = jnp.where(agg >= 1, start_tab[jnp.maximum(agg, 0) + 1], 0)

        def put(q, e, value):
            band[back + q, e - q + 2] += value

        products(begin, end, put)

    def pack(upper, lower):
        both = jnp.concatenate(
            [upper.reshape(members, share, tile), lower.reshape(members, share, tile)], axis=1)
        return both.astype(BF16)

    def piece(step, begin, size, index):
        who = lax.rem(mem + step, members)
        return pltpu.make_async_remote_copy(
            src_ref=send.at[who, pl.ds(begin, size)], dst_ref=recv.at[mem, pl.ds(begin, size)],
            send_sem=send_sem.at[step - 1], recv_sem=recv_sem.at[index, step - 1],
            device_id=(grp, who), device_id_type=MESH)

    def kept(begin, size, index):
        return pltpu.make_async_copy(
            send.at[mem, pl.ds(begin, size)], recv.at[mem, pl.ds(begin, size)], self_sem.at[index])

    def send_out(begin, size, index):
        lax.fori_loop(1, members, lambda s, _: (piece(s, begin, size, index).start(), 0)[1], 0)
        kept(begin, size, index).start()

    def turn(w, _):
        def quarter(h, _):
            a_copy(1 + 2 * w + h).wait()
            for t in range(CHUNK):
                position = 2 * CHUNK * w + CHUNK * h + t
                ap_row(position, HALO + position, own, inner_index)
            return 0

        lax.fori_loop(0, 2, quarter, 0)
        aggregate(1 + 2 * w)
        aggregate(2 + 2 * w)

        @pl.when(w >= 1)
        def _():
            for o in range(BAND):
                send[:, (w - 1) * BAND + o] = pack(band[1 + 2 * w, o], band[2 + 2 * w, o])
            send_out((w - 1) * BAND, BAND, w - 1)
        return 0

    lax.fori_loop(0, inner // (2 * CHUNK), turn, 0)

    for c in (0, cap // CHUNK - 1):
        a_copy(c).wait()
    for r in range(HALO):
        to_next(r).wait_recv()
        to_prev(r).wait_recv()

    def edge_rows(h, _):
        for t in range(CHUNK):
            place = h * CHUNK + t
            row = jnp.where(place < HALO, place, jnp.maximum(n - 2 * HALO + place, 0))
            ap_row(inner + place, row, edge, edge_index)
        return 0

    lax.fori_loop(0, 2 * HALO // CHUNK, edge_rows, 0)
    aggregate(gmax - 1)

    def put_near(q, e, value):
        near[q, e] = value

    products(start_tab[0], start_tab[1], put_near)
    shift = jnp.clip(gmax - ga, 0, gmax - 1) + 1
    for o in range(BAND):
        upper, lower = band[shift, o], band[shift + 1, o]
        if 1 <= o <= WIDE:
            upper = upper + near[1, o - 1]
        if o < WIDE:
            lower = lower + near[2, o]
        send[:, (pairs - 2) * BAND + o] = pack(upper, lower)
    send_out((pairs - 2) * BAND, BAND, pairs - 2)
    for o in range(BAND):
        send[:, (pairs - 1) * BAND + o] = pack(band[gmax - 1, o], band[gmax, o])
    send_out((pairs - 1) * BAND, BAND, pairs - 1)
    for e in range(WIDE):
        send[:, spill + e] = pack(near[0, e], band[gmax + 1, e] + jnp.where(ga == 1, near[2, e], 0.0))
    send_out(spill, WIDE, pairs)

    def arrive(begin, size, index):
        lax.fori_loop(1, members, lambda s, _: (piece(s, begin, size, index).wait_recv(), 0)[1], 0)
        kept(begin, size, index).wait()

    def unpack(u, _):
        arrive(u * BAND, BAND, u)

        def body(who, _):
            for o in range(BAND):
                both = recv[who, u * BAND + o].astype(F32)
                wide[who * slots + 2 * u, o] = both[:share]
                wide[who * slots + 2 * u + 1, o] = both[share:]
            return 0

        return lax.fori_loop(0, members, body, 0)

    lax.fori_loop(0, pairs, unpack, 0)
    arrive(spill, WIDE, pairs)

    def unpack_spill(who, _):
        for e in range(WIDE):
            both = recv[who, spill + e].astype(F32)
            wide[who * slots + gmax, e + 2] = both[:share]
            wide[who * slots + gmax + 1, e] = both[share:]
        return 0

    lax.fori_loop(0, members, unpack_spill, 0)

    def add_spill(who, _):
        base, after = who * slots, (who + 1) * slots
        count = aggs[grp, who]
        for e in range(WIDE):
            wide[after + gmax - 4, e] += wide[base + gmax + 1, e]
            value = wide[after + gmax, e + 2]
            wide[base + gmax - 1, e + 2] += value
            wide[base + gmax - 4, e + 2] += jnp.where(count == 1, value, 0.0)
            wide[base + gmax - 3, e + 2] += jnp.where(count == 2, value, 0.0)
        return 0

    lax.fori_loop(0, members - 1, add_spill, 0)

    def z_pack(h, _):
        for way, base in ((0, coarse - fmax), (1, 0)):
            one = wide[row_tab[jnp.minimum(base + 2 * h, coarse - 1)]]
            two = wide[row_tab[jnp.minimum(base + 2 * h + 1, coarse - 1)]]
            for o in range(BAND):
                zsend[way, h * BAND + o] = jnp.concatenate([one[o], two[o]], axis=0).astype(BF16)
        return 0

    lax.fori_loop(0, (fmax + 1) // 2, z_pack, 0)
    ways = [
        pltpu.make_async_remote_copy(
            src_ref=zsend.at[way], dst_ref=zrecv.at[way], send_sem=z_send.at[way], recv_sem=z_recv.at[way],
            device_id=(group, mem), device_id_type=MESH)
        for way, group in ((0, up), (1, down))
    ]
    for way in ways:
        way.start()

    take_lower = flows[0, down]
    take_upper = flows[1, up]
    give_back = flows[1, grp]
    middle = coarse - flows[0, grp] - give_back
    foreign = members * slots
    wide[foreign + 2 * fmax + 2] = jnp.zeros((BAND, share, tile), F32)

    def gather(slot):
        row = jnp.where(slot < take_lower, slot - take_lower,
                        jnp.where(slot < take_lower + middle, give_back + slot - take_lower,
                                  coarse + slot - take_lower - middle))
        native = row_tab[jnp.clip(row, 0, coarse - 1)]
        where = jnp.where(row < 0, foreign + fmax + row,
                          jnp.where(row >= coarse, foreign + fmax + 1 + row - coarse, native))
        live = slot < take_lower + middle + take_upper
        index = jnp.where(live, where, foreign + 2 * fmax + 2)
        outv[slot] = wide[jnp.clip(index, 0, foreign + 2 * fmax + 2)]

    def gather_all(begin, end):
        def body(h, _):
            for t in range(4):
                gather(jnp.minimum(begin + 4 * h + t, end - 1))
            return 0
        lax.fori_loop(0, (end - begin + 3) // 4, body, 0)

    def out_copy(begin, end, index):
        return pltpu.make_async_copy(
            outv.at[pl.ds(begin, end - begin)], out_hbm.at[pl.ds(begin, end - begin)], out_sem.at[index])

    tail = 1 + coarse - 2 * fmax
    gather_all(fmax, tail)
    out_copy(fmax, tail, 0).start()
    for way in ways:
        way.wait()

    def z_unpack(h, _):
        for way, base in ((0, foreign), (1, foreign + fmax + 1)):
            for o in range(BAND):
                both = zrecv[way, h * BAND + o].astype(F32)
                wide[base + 2 * h, o] = both[:share]
                wide[base + 2 * h + 1, o] = both[share:]
        return 0

    lax.fori_loop(0, (fmax + 1) // 2, z_unpack, 0)
    for e in range(WIDE):
        wide[foreign + fmax - 1, e + 2] += wide[gmax, e + 2]
        wide[foreign + fmax + 1, e] += wide[foreign - 1, e]
    gather_all(0, fmax)
    gather_all(tail, out_cap)
    out_copy(0, fmax, 1).start()
    out_copy(tail, out_cap, 2).start()
    lax.fori_loop(1, members, lambda s, _: (piece(s, 0, total, 0).wait_send(), 0)[1], 0)
    for r in range(HALO):
        to_next(r).wait_send()
        to_prev(r).wait_send()
    for begin, end, index in ((fmax, tail, 0), (0, fmax, 1), (tail, out_cap, 2)):
        out_copy(begin, end, index).wait()


def local(a_tiles, p_tiles, a_offsets, agg_counts, row_counts, flows):
    cap, _, tile, _ = a_tiles.shape
    groups, members = lax.axis_size("grp"), lax.axis_size("mem")
    gmax = cap // 4
    pairs = gmax // 2
    coarse = members * gmax // 2
    fmax = coarse // 8
    share = tile // members
    pieces = pairs * BAND + WIDE
    out_cap = coarse + 2 * fmax - 2
    handed = (fmax + 1) // 2 * BAND
    smem = pl.BlockSpec(memory_space=pltpu.SMEM)
    hbm = pl.BlockSpec(memory_space=pl.ANY)
    return pl.pallas_call(
        functools.partial(fused, (groups, members, cap, tile)),
        out_shape=jax.ShapeDtypeStruct((out_cap, BAND, share, tile), F32),
        in_specs=[hbm, hbm, smem, smem, smem, smem],
        out_specs=hbm,
        scratch_shapes=[
            pltpu.VMEM((cap, KA, tile, tile), BF16),
            pltpu.VMEM((WIDE * cap + 2, tile, tile), BF16),
            pltpu.VMEM((WIDE * 6 * HALO + 2, tile, tile), BF16),
            pltpu.VMEM((HALO * KP, tile, tile), BF16),
            pltpu.VMEM((cap, WIDE, tile, tile), BF16),
            pltpu.VMEM((cap + 1, KP * tile, tile), BF16),
            pltpu.VMEM((gmax + 2, BAND, tile, tile), F32),
            pltpu.VMEM((KP, WIDE, tile, tile), F32),
            pltpu.VMEM((members, pieces, 2 * share, tile), BF16),
            pltpu.VMEM((members, pieces, 2 * share, tile), BF16),
            pltpu.VMEM((members * (gmax + 2) + 2 * fmax + 3, BAND, share, tile), F32),
            pltpu.VMEM((out_cap, BAND, share, tile), F32),
            pltpu.VMEM((2, handed, 2 * share, tile), BF16),
            pltpu.VMEM((2, handed, 2 * share, tile), BF16),
            pltpu.SMEM((gmax + 2,), jnp.int32),
            pltpu.SMEM((cap,), jnp.int32),
            pltpu.SMEM((coarse,), jnp.int32),
            pltpu.SemaphoreType.DMA((cap // CHUNK,)),
            pltpu.SemaphoreType.DMA,
            pltpu.SemaphoreType.DMA((2 * HALO,)),
            pltpu.SemaphoreType.DMA((2 * HALO,)),
            pltpu.SemaphoreType.DMA((members - 1,)),
            pltpu.SemaphoreType.DMA((pairs + 1, members - 1)),
            pltpu.SemaphoreType.DMA((pairs + 1,)),
            pltpu.SemaphoreType.DMA((2,)),
            pltpu.SemaphoreType.DMA((2,)),
            pltpu.SemaphoreType.DMA((3,)),
        ],
        compiler_params=pltpu.CompilerParams(
            collective_id=0, has_side_effects=True, vmem_limit_bytes=62 * 1024 * 1024),
        cost_estimate=pl.CostEstimate(flops=7_500_000_000, bytes_accessed=20_000_000, transcendentals=0),
    )(a_tiles, p_tiles, a_offsets.T, agg_counts, row_counts, flows.T)


def solution(mesh):
    placed = (
        P(("grp", "mem"), None, None, None),
        P(("grp", "mem"), None, None, None),
        P(("grp", "mem"), None),
        P(),
        P(),
        P(),
    )
    return jax.shard_map(
        local, mesh=mesh, in_specs=placed, out_specs=P("grp", None, "mem", None), check_vma=False
    )
```

```python
import functools

import jax
import jax.numpy as jnp
from jax import lax
from jax.experimental import pallas as pl
from jax.experimental.pallas import tpu as pltpu
from jax.sharding import PartitionSpec as P

MESH = pl.DeviceIdType.MESH
F32 = jnp.float32
BF16 = jnp.bfloat16
KA = 7
KP = 3
BAND = 7
HALO = 4
WIDE = 5
STRIDE = 6
LEAD = STRIDE - KP
CHUNK = 4
LONG = 8
EARLY = 8


def fused(sizes, a_hbm, p_hbm, offs, aggs, rows, flows, outv,
          a_early, a_all, own, edge, ghost_out, ap, pt, band, near, send, recv, foreign, zsend, zrecv,
          start_tab, agg_tab, slot_tab, who_tab,
          a_sem, p_sem, halo_send, halo_recv, send_sem, recv_sem, self_sem, z_send, z_recv):
    groups, members, cap, tile = sizes
    gmax = cap // 4
    pairs = gmax // 2
    coarse = members * gmax // 2
    fmax = coarse // 8
    out_cap = outv.shape[0]
    share = tile // members
    side = 2 if members == 4 else 4
    spill = pairs * BAND
    total = spill + WIDE
    inner = cap - 2 * HALO
    grp = lax.axis_index("grp")
    mem = lax.axis_index("mem")
    up, down = lax.rem(grp + 1, groups), lax.rem(grp + groups - 1, groups)
    last = (mem == members - 1).astype(jnp.int32)
    first = (mem == 0).astype(jnp.int32)
    next_dev = (lax.rem(grp + last, groups), lax.rem(mem + 1, members))
    prev_dev = (lax.rem(grp + groups - first, groups), lax.rem(mem + members - 1, members))

    def p_copy(r):
        return pltpu.make_async_copy(p_hbm.at[pl.ds(KP * r, KP)], own.at[pl.ds(STRIDE * r + LEAD, KP)], p_sem)

    early = pltpu.make_async_copy(
        a_hbm.at[pl.ds(KA * HALO, KA * EARLY)], a_early.at[pl.ds(0, KA * EARLY)], a_sem.at[0])
    whole_a = pltpu.make_async_copy(a_hbm, a_all.at[pl.ds(0, KA * cap)], a_sem.at[1])
    lax.fori_loop(0, cap, lambda r, _: (p_copy(r).start(), 0)[1], 0)
    early.start()
    whole_a.start()

    barrier = pltpu.get_barrier_semaphore()

    def greet(step, _):
        pl.semaphore_signal(barrier, inc=1, device_id=(grp, lax.rem(mem + step, members)), device_id_type=MESH)
        return 0

    lax.fori_loop(1, members, greet, 0)
    for device in ((up, mem), (down, mem), next_dev, prev_dev):
        pl.semaphore_signal(barrier, inc=1, device_id=device, device_id_type=MESH)

    n = rows[grp, mem]
    ga = aggs[grp, mem]

    def fill_agg(r, carry):
        agg, rest = carry
        agg_tab[r] = agg
        rest = rest + ga
        step = (rest >= n).astype(jnp.int32)
        return jnp.minimum(agg + step, gmax), rest - step * n

    lax.fori_loop(0, cap + 1, fill_agg, (jnp.int32(0), jnp.int32(0)))

    def fill_start(a, carry):
        q, rest = carry
        start_tab[a] = jnp.where(a > ga, 2 * cap, q + (rest > 0).astype(jnp.int32))
        rest = rest + n
        for _ in range(LONG):
            step = (rest >= ga).astype(jnp.int32)
            q, rest = q + step, rest - step * ga
        return q, rest

    lax.fori_loop(0, gmax + 3, fill_start, (jnp.int32(0), jnp.int32(0)))

    def fill_row(c, carry):
        who, place = carry
        count = aggs[grp, who]
        slot = jnp.where(place < 2, gmax - 4 + place,
                         jnp.where(place >= count - 2, gmax + place - count, gmax - 2 + place - count))
        slot_tab[c] = jnp.clip(slot, 0, gmax - 1)
        who_tab[c] = who
        done = (place + 1 >= count).astype(jnp.int32)
        return jnp.minimum(who + done, members - 1), (1 - done) * (place + 1)

    lax.fori_loop(0, coarse, fill_row, (jnp.int32(0), jnp.int32(0)))

    blank = jnp.zeros((tile, tile), BF16)

    def blank_row(table):
        def body(r, _):
            for e in range(LEAD):
                table[STRIDE * r + e] = blank
            return 0
        return body

    lax.fori_loop(0, cap + 1, blank_row(own), 0)
    lax.fori_loop(0, 6 * HALO + 1, blank_row(edge), 0)
    pt[cap] = jnp.zeros((KP * tile, tile), BF16)
    a_early[KA * EARLY] = blank
    a_all[KA * cap] = blank

    def blank_band(s, _):
        band[s] = jnp.zeros((BAND, members, share, tile), F32)
        return 0

    lax.fori_loop(0, gmax + 2, blank_band, 0)

    whole = own.at[pl.ds(0, KP * cap)]
    pltpu.make_async_copy(whole, whole, p_sem).wait()

    def to_next(r):
        return pltpu.make_async_remote_copy(
            src_ref=ghost_out.at[pl.ds(KP * r, KP)], dst_ref=edge.at[pl.ds(STRIDE * r + LEAD, KP)],
            send_sem=halo_send.at[r], recv_sem=halo_recv.at[r], device_id=next_dev, device_id_type=MESH)

    def to_prev(r):
        return pltpu.make_async_remote_copy(
            src_ref=own.at[pl.ds(STRIDE * r + LEAD, KP)],
            dst_ref=edge.at[pl.ds(STRIDE * (5 * HALO + r) + LEAD, KP)],
            send_sem=halo_send.at[HALO + r], recv_sem=halo_recv.at[HALO + r],
            device_id=prev_dev, device_id_type=MESH)

    def halo_out():
        for r in range(HALO):
            for q in range(KP):
                ghost_out[KP * r + q] = own[STRIDE * jnp.maximum(n - HALO + r, 0) + LEAD + q]
        pl.semaphore_wait(barrier, members - 1 + 4)
        for r in range(HALO):
            to_next(r).start()
            to_prev(r).start()
        for r in range(2 * HALO):
            for q in range(KP):
                edge[STRIDE * (HALO + r) + LEAD + q] = own[STRIDE * r + LEAD + q]
                edge[STRIDE * (3 * HALO + r) + LEAD + q] = own[STRIDE * jnp.maximum(n - 2 * HALO + r, 0) + LEAD + q]

    def ap_pair(position, row, a_ref, a_first, blank_tile, table, index_of):
        agg = agg_tab[row]
        begin, end, beyond = start_tab[agg], start_tab[agg + 1], start_tab[agg + 2]
        window = 2 * HALO + 2
        bases = []
        for w in range(window):
            target = row - HALO + w
            ahead = ((target >= end).astype(jnp.int32) + (target >= beyond).astype(jnp.int32)
                     - (target < begin).astype(jnp.int32))
            bases.append(STRIDE * index_of(target) + LEAD - 1 - ahead)

        def tile_at(line, offset):
            base = KA * (line - a_first)
            if offset == 0:
                return a_ref[base]
            index = jnp.int32(blank_tile)
            if abs(offset) <= HALO:
                for k in range(1, KA):
                    index = jnp.where(offs[k, line] == offset, base + k, index)
            return a_ref[index]

        lhs = jnp.concatenate(
            [jnp.concatenate([tile_at(row, w - HALO), tile_at(row + 1, w - HALO - 1)], axis=0)
             for w in range(window)], axis=1)
        same = agg_tab[row + 1] == agg
        lower = []
        for low, from_w in ((0, 0), (2, 0), (4, HALO)):
            rhs = jnp.concatenate(
                [jnp.concatenate([table[b + low], table[b + low + 1]], axis=1) for b in bases[from_w:]], axis=0)
            out = jnp.dot(lhs[:, from_w * tile:], rhs, preferred_element_type=F32)
            for e in (0, 1):
                if low + e < WIDE:
                    ap[position, low + e] = out[:tile, e * tile:(e + 1) * tile].astype(BF16)
                lower.append(out[tile:, e * tile:(e + 1) * tile])
        for e in range(WIDE):
            ap[position + 1, e] = jnp.where(same, lower[e], lower[e + 1]).astype(BF16)
        for t in (0, 1):
            for q in range(KP):
                pt[position + t, pl.ds(q * tile, tile), :] = own[STRIDE * (row + t) + LEAD + q].T

    def inner_index(target):
        return jnp.clip(target, 0, cap - 1)

    def edge_index(target):
        from_end = 5 * HALO + target - n
        index = jnp.where(jnp.logical_or(target >= n, target >= 2 * HALO), from_end, HALO + target)
        return jnp.clip(index, 0, 6 * HALO - 1)

    def place_of(row):
        place = jnp.where(row < HALO, inner + row, jnp.where(row >= n - HALO, cap - n + row, row - HALO))
        return jnp.clip(place, 0, cap - 1)

    def products(begin, end, put):
        left, right = [], []
        for t in range(LONG):
            live = begin + t < end
            place = place_of(begin + t)
            left.append(jnp.where(live, place, cap))
            right.append(jnp.where(live, place, 0))
        lhs = jnp.concatenate([pt[i] for i in left], axis=1)
        for low, high in ((0, 2), (2, 4), (4, 5)):
            rhs = jnp.concatenate(
                [jnp.concatenate([ap[i, e] for e in range(low, high)], axis=1) for i in right], axis=0)
            out = jnp.dot(lhs, rhs, preferred_element_type=F32)
            for e in range(low, high):
                for q in range(KP):
                    part = out[q * tile:(q + 1) * tile, (e - low) * tile:(e - low + 1) * tile]
                    put(q, e, part.reshape(members, share, tile))

    def aggregate(back):
        agg = back + ga - gmax
        begin = start_tab[jnp.maximum(agg, 0)]
        end = jnp.where(agg >= 1, start_tab[jnp.maximum(agg, 0) + 1], 0)

        def put(q, e, value):
            band[back + q, e - q + 2] += value

        products(begin, end, put)

    def pack(upper, lower):
        return jnp.concatenate([upper, lower], axis=1).astype(BF16)

    def piece(step, begin, size, index):
        away = lax.rem(step * 7, members)
        who = (lax.rem(mem // side + away // side, side) * side
               + lax.rem(lax.rem(mem, side) + lax.rem(away, side), side))
        return pltpu.make_async_remote_copy(
            src_ref=send.at[who, pl.ds(begin, size)], dst_ref=recv.at[mem, pl.ds(begin, size)],
            send_sem=send_sem.at[step - 1], recv_sem=recv_sem.at[index, step - 1],
            device_id=(grp, who), device_id_type=MESH)

    def kept(begin, size, index):
        return pltpu.make_async_copy(
            send.at[mem, pl.ds(begin, size)], recv.at[mem, pl.ds(begin, size)], self_sem.at[index])

    def send_out(begin, size, index):
        lax.fori_loop(1, members, lambda s, _: (piece(s, begin, size, index).start(), 0)[1], 0)
        kept(begin, size, index).start()

    def quarter(position, a_ref, a_first, blank_tile):
        for t in range(0, CHUNK, 2):
            ap_pair(position + t, HALO + position + t, a_ref, a_first, blank_tile, own, inner_index)

    early.wait()
    lax.fori_loop(0, EARLY // CHUNK, lambda h, _: (quarter(CHUNK * h, a_early, HALO, KA * EARLY), 0)[1], 0)
    halo_out()
    aggregate(1)
    aggregate(2)
    whole_a.wait()

    def turn(w, _):
        lax.fori_loop(0, 2, lambda h, _: (quarter(2 * CHUNK * w + CHUNK * h, a_all, 0, KA * cap), 0)[1], 0)
        aggregate(1 + 2 * w)
        aggregate(2 + 2 * w)
        for o in range(BAND):
            send[:, (w - 1) * BAND + o] = pack(band[1 + 2 * w, o], band[2 + 2 * w, o])
        send_out((w - 1) * BAND, BAND, w - 1)
        return 0

    lax.fori_loop(1, inner // (2 * CHUNK), turn, 0)

    for r in range(HALO):
        to_next(r).wait_recv()
        to_prev(r).wait_recv()

    def edge_rows(h, _):
        for t in range(0, CHUNK, 2):
            place = h * CHUNK + t
            row = jnp.where(place < HALO, place, jnp.maximum(n - 2 * HALO + place, 0))
            ap_pair(inner + place, row, a_all, 0, KA * cap, edge, edge_index)
        return 0

    lax.fori_loop(0, 2 * HALO // CHUNK, edge_rows, 0)
    aggregate(gmax - 1)

    def put_near(q, e, value):
        near[q, e] = value

    products(start_tab[0], start_tab[1], put_near)
    shift = jnp.clip(gmax - ga, 0, gmax - 1) + 1
    for o in range(BAND):
        upper, lower = band[shift, o], band[shift + 1, o]
        if 1 <= o <= WIDE:
            upper = upper + near[1, o - 1]
        if o < WIDE:
            lower = lower + near[2, o]
        send[:, (pairs - 2) * BAND + o] = pack(upper, lower)
    send_out((pairs - 2) * BAND, BAND, pairs - 2)
    for o in range(BAND):
        send[:, (pairs - 1) * BAND + o] = pack(band[gmax - 1, o], band[gmax, o])
    send_out((pairs - 1) * BAND, BAND, pairs - 1)
    for e in range(WIDE):
        send[:, spill + e] = pack(near[0, e], band[gmax + 1, e] + jnp.where(ga == 1, near[2, e], 0.0))
    send_out(spill, WIDE, pairs)

    def arrive(begin, size, index):
        lax.fori_loop(1, members, lambda s, _: (piece(s, begin, size, index).wait_recv(), 0)[1], 0)
        kept(begin, size, index).wait()

    def unpack(u, _):
        arrive(u * BAND, BAND, u)

        def body(who, _):
            for o in range(BAND):
                both = recv[who, u * BAND + o].astype(F32)
                band[2 * u, o, who] = both[:share]
                band[2 * u + 1, o, who] = both[share:]
            return 0

        return lax.fori_loop(0, members, body, 0)

    lax.fori_loop(0, pairs, unpack, 0)
    arrive(spill, WIDE, pairs)

    def unpack_spill(who, _):
        for e in range(WIDE):
            both = recv[who, spill + e].astype(F32)
            band[gmax, e + 2, who] = both[:share]
            band[gmax + 1, e, who] = both[share:]
        return 0

    lax.fori_loop(0, members, unpack_spill, 0)

    def add_spill(who, _):
        here, after = who, who + 1
        count = aggs[grp, who]
        for e in range(WIDE):
            band[gmax - 4, e, after] += band[gmax + 1, e, here]
            value = band[gmax, e + 2, after]
            band[gmax - 1, e + 2, here] += value
            band[gmax - 4, e + 2, here] += jnp.where(count == 1, value, 0.0)
            band[gmax - 3, e + 2, here] += jnp.where(count == 2, value, 0.0)
        return 0

    lax.fori_loop(0, members - 1, add_spill, 0)

    def coarse_row(row):
        row = jnp.clip(row, 0, coarse - 1)
        slot, who = slot_tab[row], who_tab[row]
        return [band[slot, o, who] for o in range(BAND)]

    def z_pack(h, _):
        for way, base in ((0, coarse - fmax), (1, 0)):
            one, two = coarse_row(base + 2 * h), coarse_row(base + 2 * h + 1)
            for o in range(BAND):
                zsend[way, h * BAND + o] = jnp.concatenate([one[o], two[o]], axis=0).astype(BF16)
        return 0

    lax.fori_loop(0, (fmax + 1) // 2, z_pack, 0)
    ways = [
        pltpu.make_async_remote_copy(
            src_ref=zsend.at[way], dst_ref=zrecv.at[way], send_sem=z_send.at[way], recv_sem=z_recv.at[way],
            device_id=(group, mem), device_id_type=MESH)
        for way, group in ((0, up), (1, down))
    ]
    for way in ways:
        way.start()

    take_lower = flows[0, down]
    take_upper = flows[1, up]
    give_back = flows[1, grp]
    middle = coarse - flows[0, grp] - give_back
    foreign[2 * fmax + 2] = jnp.zeros((BAND, share, tile), F32)

    def place(slot):
        return jnp.where(slot < take_lower, slot - take_lower,
                         jnp.where(slot < take_lower + middle, give_back + slot - take_lower,
                                   coarse + slot - take_lower - middle))

    def in_middle(slot):
        for o, value in enumerate(coarse_row(place(slot))):
            outv[slot, o] = value

    def at_end(slot):
        row = place(slot)
        live = slot < take_lower + middle + take_upper
        native = jnp.logical_and(live, jnp.logical_and(row >= 0, row < coarse))
        index = jnp.where(live, jnp.where(row < 0, fmax + row, fmax + 1 + row - coarse), 2 * fmax + 2)
        other = foreign[jnp.clip(index, 0, 2 * fmax + 2)]
        for o, value in enumerate(coarse_row(row)):
            outv[slot, o] = jnp.where(native, value, other[o])

    def gather_all(fill, begin, end):
        def body(h, _):
            for t in range(4):
                fill(jnp.minimum(begin + 4 * h + t, end - 1))
            return 0
        lax.fori_loop(0, (end - begin + 3) // 4, body, 0)

    tail = 1 + coarse - 2 * fmax
    gather_all(in_middle, fmax, tail)
    for way in ways:
        way.wait()

    def z_unpack(h, _):
        for way, base in ((0, 0), (1, fmax + 1)):
            for o in range(BAND):
                both = zrecv[way, h * BAND + o].astype(F32)
                foreign[base + 2 * h, o] = both[:share]
                foreign[base + 2 * h + 1, o] = both[share:]
        return 0

    lax.fori_loop(0, (fmax + 1) // 2, z_unpack, 0)
    for e in range(WIDE):
        foreign[fmax - 1, e + 2] += band[gmax, e + 2, 0]
        foreign[fmax + 1, e] += band[gmax + 1, e, members - 1]
    gather_all(at_end, 0, fmax)
    gather_all(at_end, tail, out_cap)
    lax.fori_loop(1, members, lambda s, _: (piece(s, 0, total, 0).wait_send(), 0)[1], 0)
    for r in range(HALO):
        to_next(r).wait_send()
        to_prev(r).wait_send()


def write_out(held, out_hbm, sem):
    copy = pltpu.make_async_copy(held, out_hbm, sem)
    copy.start()
    copy.wait()


def local(a_tiles, p_tiles, a_offsets, agg_counts, row_counts, flows):
    cap, _, tile, _ = a_tiles.shape
    groups, members = lax.axis_size("grp"), lax.axis_size("mem")
    gmax = cap // 4
    pairs = gmax // 2
    coarse = members * gmax // 2
    fmax = coarse // 8
    share = tile // members
    pieces = pairs * BAND + WIDE
    out_cap = coarse + 2 * fmax - 2
    handed = (fmax + 1) // 2 * BAND
    smem = pl.BlockSpec(memory_space=pltpu.SMEM)
    hbm = pl.BlockSpec(memory_space=pl.ANY)
    vmem = pl.BlockSpec(memory_space=pltpu.VMEM)
    held = pl.pallas_call(
        functools.partial(fused, (groups, members, cap, tile)),
        out_shape=pltpu.VMEM((out_cap, BAND, share, tile), F32),
        in_specs=[hbm, hbm, smem, smem, smem, smem],
        out_specs=vmem,
        scratch_shapes=[
            pltpu.VMEM((KA * EARLY + 1, tile, tile), BF16),
            pltpu.VMEM((KA * cap + 1, tile, tile), BF16),
            pltpu.VMEM((STRIDE * cap + LEAD, tile, tile), BF16),
            pltpu.VMEM((STRIDE * 6 * HALO + LEAD, tile, tile), BF16),
            pltpu.VMEM((HALO * KP, tile, tile), BF16),
            pltpu.VMEM((cap, WIDE, tile, tile), BF16),
            pltpu.VMEM((cap + 1, KP * tile, tile), BF16),
            pltpu.VMEM((gmax + 2, BAND, members, share, tile), F32),
            pltpu.VMEM((KP, WIDE, members, share, tile), F32),
            pltpu.VMEM((members, pieces, 2 * share, tile), BF16),
            pltpu.VMEM((members, pieces, 2 * share, tile), BF16),
            pltpu.VMEM((2 * fmax + 3, BAND, share, tile), F32),
            pltpu.VMEM((2, handed, 2 * share, tile), BF16),
            pltpu.VMEM((2, handed, 2 * share, tile), BF16),
            pltpu.SMEM((gmax + 3,), jnp.int32),
            pltpu.SMEM((cap + 1,), jnp.int32),
            pltpu.SMEM((coarse,), jnp.int32),
            pltpu.SMEM((coarse,), jnp.int32),
            pltpu.SemaphoreType.DMA((2,)),
            pltpu.SemaphoreType.DMA,
            pltpu.SemaphoreType.DMA((2 * HALO,)),
            pltpu.SemaphoreType.DMA((2 * HALO,)),
            pltpu.SemaphoreType.DMA((members - 1,)),
            pltpu.SemaphoreType.DMA((pairs + 1, members - 1)),
            pltpu.SemaphoreType.DMA((pairs + 1,)),
            pltpu.SemaphoreType.DMA((2,)),
            pltpu.SemaphoreType.DMA((2,)),
        ],
        compiler_params=pltpu.CompilerParams(
            collective_id=0, has_side_effects=True, vmem_limit_bytes=58 * 1024 * 1024),
        cost_estimate=pl.CostEstimate(flops=7_500_000_000, bytes_accessed=20_000_000, transcendentals=0),
    )(a_tiles.reshape(cap * KA, tile, tile), p_tiles.reshape(cap * KP, tile, tile), a_offsets.T,
      agg_counts, row_counts, flows.T)
    return pl.pallas_call(
        write_out,
        out_shape=jax.ShapeDtypeStruct((out_cap, BAND, share, tile), F32),
        in_specs=[vmem],
        out_specs=hbm,
        scratch_shapes=[pltpu.SemaphoreType.DMA],
        cost_estimate=pl.CostEstimate(flops=0, bytes_accessed=6_800_000, transcendentals=0),
    )(held)


def solution(mesh):
    placed = (
        P(("grp", "mem"), None, None, None),
        P(("grp", "mem"), None, None, None),
        P(("grp", "mem"), None),
        P(),
        P(),
        P(),
    )
    return jax.shard_map(
        local, mesh=mesh, in_specs=placed, out_specs=P("grp", None, "mem", None), check_vma=False
    )
```

```python
import functools

import jax
import jax.numpy as jnp
from jax import lax
from jax.experimental import pallas as pl
from jax.experimental.pallas import tpu as pltpu
from jax.sharding import PartitionSpec as P

MESH = pl.DeviceIdType.MESH
F32 = jnp.float32
BF16 = jnp.bfloat16
KA = 7
KP = 3
BAND = 7
HALO = 4
WIDE = 5
STRIDE = 6
LEAD = STRIDE - KP
CHUNK = 4
LONG = 8
EARLY = 8


def fused(sizes, a_hbm, p_hbm, offs, aggs, rows, flows, outv,
          a_early, a_mid, a_all, own, edge, ghost_out, ap, pt, band, near, send, recv, foreign, zsend, zrecv,
          start_tab, agg_tab, slot_tab, who_tab,
          a_sem, p_sem, halo_send, halo_recv, send_sem, recv_sem, self_sem, z_send, z_recv):
    groups, members, cap, tile = sizes
    gmax = cap // 4
    pairs = gmax // 2
    coarse = members * gmax // 2
    fmax = coarse // 8
    out_cap = outv.shape[0]
    share = tile // members
    side = 2 if members == 4 else 4
    spill = pairs * BAND
    total = spill + WIDE
    inner = cap - 2 * HALO
    grp = lax.axis_index("grp")
    mem = lax.axis_index("mem")
    up, down = lax.rem(grp + 1, groups), lax.rem(grp + groups - 1, groups)
    last = (mem == members - 1).astype(jnp.int32)
    first = (mem == 0).astype(jnp.int32)
    next_dev = (lax.rem(grp + last, groups), lax.rem(mem + 1, members))
    prev_dev = (lax.rem(grp + groups - first, groups), lax.rem(mem + members - 1, members))

    def p_copy(r):
        return pltpu.make_async_copy(p_hbm.at[pl.ds(KP * r, KP)], own.at[pl.ds(STRIDE * r + LEAD, KP)], p_sem)

    def a_copy(r):
        return pltpu.make_async_copy(a_hbm.at[pl.ds(KA * r, KA)], a_all.at[pl.ds(KA * r, KA)], a_sem.at[1])

    def early_copy(r, count):
        return pltpu.make_async_copy(
            a_hbm.at[pl.ds(KA * (HALO + r), KA * count)], a_early.at[pl.ds(KA * r, KA * count)], a_sem.at[0])

    def mid_copy(r, count):
        return pltpu.make_async_copy(
            a_hbm.at[pl.ds(KA * (HALO + EARLY + r), KA * count)], a_mid.at[pl.ds(KA * r, KA * count)], a_sem.at[2])

    whole_a = pltpu.make_async_copy(a_hbm, a_all.at[pl.ds(0, KA * cap)], a_sem.at[1])
    lax.fori_loop(0, cap, lambda r, _: (p_copy(r).start(), 0)[1], 0)
    lax.fori_loop(0, EARLY, lambda r, _: (early_copy(r, 1).start(), 0)[1], 0)
    lax.fori_loop(0, EARLY, lambda r, _: (mid_copy(r, 1).start(), 0)[1], 0)
    lax.fori_loop(0, cap, lambda r, _: (a_copy(r).start(), 0)[1], 0)

    barrier = pltpu.get_barrier_semaphore()

    def greet(step, _):
        pl.semaphore_signal(barrier, inc=1, device_id=(grp, lax.rem(mem + step, members)), device_id_type=MESH)
        return 0

    lax.fori_loop(1, members, greet, 0)
    for device in ((up, mem), (down, mem), next_dev, prev_dev):
        pl.semaphore_signal(barrier, inc=1, device_id=device, device_id_type=MESH)

    n = rows[grp, mem]
    ga = aggs[grp, mem]

    def fill_agg(r, carry):
        agg, rest = carry
        agg_tab[r] = agg
        rest = rest + ga
        step = (rest >= n).astype(jnp.int32)
        return jnp.minimum(agg + step, gmax), rest - step * n

    lax.fori_loop(0, cap + 1, fill_agg, (jnp.int32(0), jnp.int32(0)))

    def fill_start(a, carry):
        q, rest = carry
        start_tab[a] = jnp.where(a > ga, 2 * cap, q + (rest > 0).astype(jnp.int32))
        rest = rest + n
        for _ in range(LONG):
            step = (rest >= ga).astype(jnp.int32)
            q, rest = q + step, rest - step * ga
        return q, rest

    lax.fori_loop(0, gmax + 3, fill_start, (jnp.int32(0), jnp.int32(0)))


    def to_next(r):
        return pltpu.make_async_remote_copy(
            src_ref=ghost_out.at[pl.ds(KP * r, KP)], dst_ref=edge.at[pl.ds(STRIDE * r + LEAD, KP)],
            send_sem=halo_send.at[r], recv_sem=halo_recv.at[r], device_id=next_dev, device_id_type=MESH)

    def to_prev(r):
        return pltpu.make_async_remote_copy(
            src_ref=p_hbm.at[pl.ds(KP * r, KP)],
            dst_ref=edge.at[pl.ds(STRIDE * (5 * HALO + r) + LEAD, KP)],
            send_sem=halo_send.at[HALO + r], recv_sem=halo_recv.at[HALO + r],
            device_id=prev_dev, device_id_type=MESH)

    pl.semaphore_wait(barrier, members - 1 + 4)
    for r in range(HALO):
        to_prev(r).start()

    blank = jnp.zeros((tile, tile), BF16)

    def blank_row(table):
        def body(r, _):
            for e in range(LEAD):
                table[STRIDE * r + e] = blank
            return 0
        return body

    lax.fori_loop(0, cap + 1, blank_row(own), 0)
    lax.fori_loop(0, 6 * HALO + 1, blank_row(edge), 0)
    pt[cap] = jnp.zeros((KP * tile, tile), BF16)
    a_early[KA * EARLY] = blank
    a_mid[KA * EARLY] = blank
    a_all[KA * cap] = blank

    def blank_band(s, _):
        band[s] = jnp.zeros((BAND, members, share, tile), F32)
        return 0

    lax.fori_loop(0, gmax + 2, blank_band, 0)

    whole = own.at[pl.ds(0, KP * cap)]
    pltpu.make_async_copy(whole, whole, p_sem).wait()
    for r in range(HALO):
        for q in range(KP):
            ghost_out[KP * r + q] = own[STRIDE * jnp.maximum(n - HALO + r, 0) + LEAD + q]
        to_next(r).start()

    def edge_table():
        for r in range(2 * HALO):
            for q in range(KP):
                edge[STRIDE * (HALO + r) + LEAD + q] = own[STRIDE * r + LEAD + q]
                edge[STRIDE * (3 * HALO + r) + LEAD + q] = own[STRIDE * jnp.maximum(n - 2 * HALO + r, 0) + LEAD + q]

    def ap_pair(position, row, a_ref, a_first, blank_tile, table, index_of):
        agg = agg_tab[row]
        begin, end, beyond = start_tab[agg], start_tab[agg + 1], start_tab[agg + 2]
        window = 2 * HALO + 2
        bases = []
        for w in range(window):
            target = row - HALO + w
            ahead = ((target >= end).astype(jnp.int32) + (target >= beyond).astype(jnp.int32)
                     - (target < begin).astype(jnp.int32))
            bases.append(STRIDE * index_of(target) + LEAD - 1 - ahead)

        def tile_at(line, offset):
            base = KA * (line - a_first)
            if offset == 0:
                return a_ref[base]
            index = jnp.int32(blank_tile)
            if abs(offset) <= HALO:
                for k in range(1, KA):
                    index = jnp.where(offs[k, line] == offset, base + k, index)
            return a_ref[index]

        lhs = jnp.concatenate(
            [jnp.concatenate([tile_at(row, w - HALO), tile_at(row + 1, w - HALO - 1)], axis=0)
             for w in range(window)], axis=1)
        same = agg_tab[row + 1] == agg
        lower = []
        for low, from_w in ((0, 0), (2, 0), (4, HALO)):
            rhs = jnp.concatenate(
                [jnp.concatenate([table[b + low], table[b + low + 1]], axis=1) for b in bases[from_w:]], axis=0)
            out = jnp.dot(lhs[:, from_w * tile:], rhs, preferred_element_type=F32)
            for e in (0, 1):
                if low + e < WIDE:
                    ap[position, low + e] = out[:tile, e * tile:(e + 1) * tile].astype(BF16)
                lower.append(out[tile:, e * tile:(e + 1) * tile])
        for e in range(WIDE):
            ap[position + 1, e] = jnp.where(same, lower[e], lower[e + 1]).astype(BF16)
        for t in (0, 1):
            for q in range(KP):
                pt[position + t, pl.ds(q * tile, tile), :] = own[STRIDE * (row + t) + LEAD + q].T

    def inner_index(target):
        return jnp.clip(target, 0, cap - 1)

    def edge_index(target):
        from_end = 5 * HALO + target - n
        index = jnp.where(jnp.logical_or(target >= n, target >= 2 * HALO), from_end, HALO + target)
        return jnp.clip(index, 0, 6 * HALO - 1)

    def place_of(row):
        place = jnp.where(row < HALO, inner + row, jnp.where(row >= n - HALO, cap - n + row, row - HALO))
        return jnp.clip(place, 0, cap - 1)

    def products(begin, end, put):
        left, right = [], []
        for t in range(LONG):
            live = begin + t < end
            place = place_of(begin + t)
            left.append(jnp.where(live, place, cap))
            right.append(jnp.where(live, place, 0))
        lhs = jnp.concatenate([pt[i] for i in left], axis=1)
        for low, high in ((0, 2), (2, 4), (4, 5)):
            rhs = jnp.concatenate(
                [jnp.concatenate([ap[i, e] for e in range(low, high)], axis=1) for i in right], axis=0)
            out = jnp.dot(lhs, rhs, preferred_element_type=F32)
            for e in range(low, high):
                for q in range(KP):
                    part = out[q * tile:(q + 1) * tile, (e - low) * tile:(e - low + 1) * tile]
                    put(q, e, part.reshape(members, share, tile))

    def aggregate(back):
        agg = back + ga - gmax
        begin = start_tab[jnp.maximum(agg, 0)]
        end = jnp.where(agg >= 1, start_tab[jnp.maximum(agg, 0) + 1], 0)

        def put(q, e, value):
            band[back + q, e - q + 2] += value

        products(begin, end, put)

    def pack(upper, lower):
        return jnp.concatenate([upper, lower], axis=1).astype(BF16)

    def piece(step, begin, size, index):
        away = lax.rem(step * 7, members)
        who = (lax.rem(mem // side + away // side, side) * side
               + lax.rem(lax.rem(mem, side) + lax.rem(away, side), side))
        return pltpu.make_async_remote_copy(
            src_ref=send.at[who, pl.ds(begin, size)], dst_ref=recv.at[mem, pl.ds(begin, size)],
            send_sem=send_sem.at[step - 1], recv_sem=recv_sem.at[index, step - 1],
            device_id=(grp, who), device_id_type=MESH)

    def kept(begin, size, index):
        return pltpu.make_async_copy(
            send.at[mem, pl.ds(begin, size)], recv.at[mem, pl.ds(begin, size)], self_sem.at[index])

    def send_out(begin, size, index):
        lax.fori_loop(1, members, lambda s, _: (piece(s, begin, size, index).start(), 0)[1], 0)
        kept(begin, size, index).start()

    def quarter(position, a_ref, a_first, blank_tile):
        for t in range(0, CHUNK, 2):
            ap_pair(position + t, HALO + position + t, a_ref, a_first, blank_tile, own, inner_index)

    def turn(w, a_ref, a_first, blank_tile):
        lax.fori_loop(
            0, 2, lambda h, _: (quarter(2 * CHUNK * w + CHUNK * h, a_ref, a_first, blank_tile), 0)[1], 0)
        aggregate(1 + 2 * w)
        aggregate(2 + 2 * w)

    def depart(w):
        for o in range(BAND):
            send[:, (w - 1) * BAND + o] = pack(band[1 + 2 * w, o], band[2 + 2 * w, o])
        send_out((w - 1) * BAND, BAND, w - 1)

    early_copy(0, EARLY).wait()
    turn(0, a_early, HALO, KA * EARLY)
    mid_copy(0, EARLY).wait()
    turn(1, a_mid, HALO + EARLY, KA * EARLY)
    depart(1)
    edge_table()
    whole_a.wait()

    def later(w, _):
        turn(w, a_all, 0, KA * cap)
        depart(w)
        return 0

    lax.fori_loop(2, inner // (2 * CHUNK), later, 0)

    for r in range(HALO):
        to_next(r).wait_recv()
        to_prev(r).wait_recv()

    def edge_rows(h, _):
        for t in range(0, CHUNK, 2):
            place = h * CHUNK + t
            row = jnp.where(place < HALO, place, jnp.maximum(n - 2 * HALO + place, 0))
            ap_pair(inner + place, row, a_all, 0, KA * cap, edge, edge_index)
        return 0

    lax.fori_loop(0, 2 * HALO // CHUNK, edge_rows, 0)
    aggregate(gmax - 1)

    def put_near(q, e, value):
        near[q, e] = value

    products(start_tab[0], start_tab[1], put_near)
    shift = jnp.clip(gmax - ga, 0, gmax - 1) + 1
    for o in range(BAND):
        upper, lower = band[shift, o], band[shift + 1, o]
        if 1 <= o <= WIDE:
            upper = upper + near[1, o - 1]
        if o < WIDE:
            lower = lower + near[2, o]
        send[:, (pairs - 2) * BAND + o] = pack(upper, lower)
    send_out((pairs - 2) * BAND, BAND, pairs - 2)
    for o in range(BAND):
        send[:, (pairs - 1) * BAND + o] = pack(band[gmax - 1, o], band[gmax, o])
    send_out((pairs - 1) * BAND, BAND, pairs - 1)
    for e in range(WIDE):
        send[:, spill + e] = pack(near[0, e], band[gmax + 1, e] + jnp.where(ga == 1, near[2, e], 0.0))
    send_out(spill, WIDE, pairs)

    def fill_row(c, carry):
        who, place = carry
        count = aggs[grp, who]
        slot = jnp.where(place < 2, gmax - 4 + place,
                         jnp.where(place >= count - 2, gmax + place - count, gmax - 2 + place - count))
        slot_tab[c] = jnp.clip(slot, 0, gmax - 1)
        who_tab[c] = who
        done = (place + 1 >= count).astype(jnp.int32)
        return jnp.minimum(who + done, members - 1), (1 - done) * (place + 1)

    lax.fori_loop(0, coarse, fill_row, (jnp.int32(0), jnp.int32(0)))

    def arrive(begin, size, index):
        lax.fori_loop(1, members, lambda s, _: (piece(s, begin, size, index).wait_recv(), 0)[1], 0)
        kept(begin, size, index).wait()

    def unpack(u, _):
        arrive(u * BAND, BAND, u)

        def body(who, _):
            for o in range(BAND):
                both = recv[who, u * BAND + o].astype(F32)
                band[2 * u, o, who] = both[:share]
                band[2 * u + 1, o, who] = both[share:]
            return 0

        return lax.fori_loop(0, members, body, 0)

    lax.fori_loop(0, pairs, unpack, 0)
    arrive(spill, WIDE, pairs)

    def unpack_spill(who, _):
        for e in range(WIDE):
            both = recv[who, spill + e].astype(F32)
            band[gmax, e + 2, who] = both[:share]
            band[gmax + 1, e, who] = both[share:]
        return 0

    lax.fori_loop(0, members, unpack_spill, 0)

    def add_spill(who, _):
        here, after = who, who + 1
        count = aggs[grp, who]
        for e in range(WIDE):
            band[gmax - 4, e, after] += band[gmax + 1, e, here]
            value = band[gmax, e + 2, after]
            band[gmax - 1, e + 2, here] += value
            band[gmax - 4, e + 2, here] += jnp.where(count == 1, value, 0.0)
            band[gmax - 3, e + 2, here] += jnp.where(count == 2, value, 0.0)
        return 0

    lax.fori_loop(0, members - 1, add_spill, 0)

    def coarse_row(row):
        row = jnp.clip(row, 0, coarse - 1)
        slot, who = slot_tab[row], who_tab[row]
        return [band[slot, o, who] for o in range(BAND)]

    def z_pack(h, _):
        for way, base in ((0, coarse - fmax), (1, 0)):
            one, two = coarse_row(base + 2 * h), coarse_row(base + 2 * h + 1)
            for o in range(BAND):
                zsend[way, h * BAND + o] = jnp.concatenate([one[o], two[o]], axis=0).astype(BF16)
        return 0

    lax.fori_loop(0, (fmax + 1) // 2, z_pack, 0)
    ways = [
        pltpu.make_async_remote_copy(
            src_ref=zsend.at[way], dst_ref=zrecv.at[way], send_sem=z_send.at[way], recv_sem=z_recv.at[way],
            device_id=(group, mem), device_id_type=MESH)
        for way, group in ((0, up), (1, down))
    ]
    for way in ways:
        way.start()

    take_lower = flows[0, down]
    take_upper = flows[1, up]
    give_back = flows[1, grp]
    middle = coarse - flows[0, grp] - give_back
    foreign[2 * fmax + 2] = jnp.zeros((BAND, share, tile), F32)

    def place(slot):
        return jnp.where(slot < take_lower, slot - take_lower,
                         jnp.where(slot < take_lower + middle, give_back + slot - take_lower,
                                   coarse + slot - take_lower - middle))

    def in_middle(slot):
        for o, value in enumerate(coarse_row(place(slot))):
            outv[slot, o] = value

    def at_end(slot):
        row = place(slot)
        live = slot < take_lower + middle + take_upper
        native = jnp.logical_and(live, jnp.logical_and(row >= 0, row < coarse))
        index = jnp.where(live, jnp.where(row < 0, fmax + row, fmax + 1 + row - coarse), 2 * fmax + 2)
        other = foreign[jnp.clip(index, 0, 2 * fmax + 2)]
        for o, value in enumerate(coarse_row(row)):
            outv[slot, o] = jnp.where(native, value, other[o])

    def gather_all(fill, begin, end):
        def body(h, _):
            for t in range(4):
                fill(jnp.minimum(begin + 4 * h + t, end - 1))
            return 0
        lax.fori_loop(0, (end - begin + 3) // 4, body, 0)

    tail = 1 + coarse - 2 * fmax
    gather_all(in_middle, fmax, tail)
    for way in ways:
        way.wait()

    def z_unpack(h, _):
        for way, base in ((0, 0), (1, fmax + 1)):
            for o in range(BAND):
                both = zrecv[way, h * BAND + o].astype(F32)
                foreign[base + 2 * h, o] = both[:share]
                foreign[base + 2 * h + 1, o] = both[share:]
        return 0

    lax.fori_loop(0, (fmax + 1) // 2, z_unpack, 0)
    for e in range(WIDE):
        foreign[fmax - 1, e + 2] += band[gmax, e + 2, 0]
        foreign[fmax + 1, e] += band[gmax + 1, e, members - 1]
    gather_all(at_end, 0, fmax)
    gather_all(at_end, tail, out_cap)
    lax.fori_loop(1, members, lambda s, _: (piece(s, 0, total, 0).wait_send(), 0)[1], 0)
    for r in range(HALO):
        to_next(r).wait_send()
        to_prev(r).wait_send()


def local(a_tiles, p_tiles, a_offsets, agg_counts, row_counts, flows):
    cap, _, tile, _ = a_tiles.shape
    groups, members = lax.axis_size("grp"), lax.axis_size("mem")
    gmax = cap // 4
    pairs = gmax // 2
    coarse = members * gmax // 2
    fmax = coarse // 8
    share = tile // members
    pieces = pairs * BAND + WIDE
    out_cap = coarse + 2 * fmax - 2
    handed = (fmax + 1) // 2 * BAND
    smem = pl.BlockSpec(memory_space=pltpu.SMEM)
    hbm = pl.BlockSpec(memory_space=pl.ANY)
    vmem = pl.BlockSpec(memory_space=pltpu.VMEM)
    return pl.pallas_call(
        functools.partial(fused, (groups, members, cap, tile)),
        out_shape=pltpu.VMEM((out_cap, BAND, share, tile), F32),
        in_specs=[hbm, hbm, smem, smem, smem, smem],
        out_specs=vmem,
        scratch_shapes=[
            pltpu.VMEM((KA * EARLY + 1, tile, tile), BF16),
            pltpu.VMEM((KA * EARLY + 1, tile, tile), BF16),
            pltpu.VMEM((KA * cap + 1, tile, tile), BF16),
            pltpu.VMEM((STRIDE * cap + LEAD, tile, tile), BF16),
            pltpu.VMEM((STRIDE * 6 * HALO + LEAD, tile, tile), BF16),
            pltpu.VMEM((HALO * KP, tile, tile), BF16),
            pltpu.VMEM((cap, WIDE, tile, tile), BF16),
            pltpu.VMEM((cap + 1, KP * tile, tile), BF16),
            pltpu.VMEM((gmax + 2, BAND, members, share, tile), F32),
            pltpu.VMEM((KP, WIDE, members, share, tile), F32),
            pltpu.VMEM((members, pieces, 2 * share, tile), BF16),
            pltpu.VMEM((members, pieces, 2 * share, tile), BF16),
            pltpu.VMEM((2 * fmax + 3, BAND, share, tile), F32),
            pltpu.VMEM((2, handed, 2 * share, tile), BF16),
            pltpu.VMEM((2, handed, 2 * share, tile), BF16),
            pltpu.SMEM((gmax + 3,), jnp.int32),
            pltpu.SMEM((cap + 1,), jnp.int32),
            pltpu.SMEM((coarse,), jnp.int32),
            pltpu.SMEM((coarse,), jnp.int32),
            pltpu.SemaphoreType.DMA((3,)),
            pltpu.SemaphoreType.DMA,
            pltpu.SemaphoreType.DMA((2 * HALO,)),
            pltpu.SemaphoreType.DMA((2 * HALO,)),
            pltpu.SemaphoreType.DMA((members - 1,)),
            pltpu.SemaphoreType.DMA((pairs + 1, members - 1)),
            pltpu.SemaphoreType.DMA((pairs + 1,)),
            pltpu.SemaphoreType.DMA((2,)),
            pltpu.SemaphoreType.DMA((2,)),
        ],
        compiler_params=pltpu.CompilerParams(
            collective_id=0, has_side_effects=True, vmem_limit_bytes=58 * 1024 * 1024),
        cost_estimate=pl.CostEstimate(flops=7_500_000_000, bytes_accessed=20_000_000, transcendentals=0),
    )(a_tiles.reshape(cap * KA, tile, tile), p_tiles.reshape(cap * KP, tile, tile), a_offsets.T,
      agg_counts, row_counts, flows.T)


def solution(mesh):
    placed = (
        P(("grp", "mem"), None, None, None),
        P(("grp", "mem"), None, None, None),
        P(("grp", "mem"), None),
        P(),
        P(),
        P(),
    )
    return jax.shard_map(
        local, mesh=mesh, in_specs=placed, out_specs=P("grp", None, "mem", None), check_vma=False
    )
```

```python
import functools

import jax
import jax.numpy as jnp
from jax import lax
from jax.experimental import pallas as pl
from jax.experimental.pallas import tpu as pltpu
from jax.sharding import PartitionSpec as P

MESH = pl.DeviceIdType.MESH
F32 = jnp.float32
BF16 = jnp.bfloat16
KA = 7
KP = 3
BAND = 7
HALO = 4
WIDE = 5
STRIDE = 6
LEAD = STRIDE - KP
CHUNK = 4
LONG = 8
EARLY = 8


def fused(sizes, a_hbm, p_hbm, offs, aggs, rows, flows, outv,
          a_early, a_mid, a_all, own, edge, ghost_out, ap, pt, unit, band, near, send, recv, foreign, zsend, zrecv,
          start_tab, agg_tab, slot_tab, who_tab,
          a_sem, p_sem, halo_send, halo_recv, send_sem, recv_sem, self_sem, z_send, z_recv):
    groups, members, cap, tile = sizes
    gmax = cap // 4
    pairs = gmax // 2
    coarse = members * gmax // 2
    fmax = coarse // 8
    out_cap = outv.shape[0]
    share = tile // members
    side = 2 if members == 4 else 4
    spill = pairs * BAND
    total = spill + WIDE
    inner = cap - 2 * HALO
    grp = lax.axis_index("grp")
    mem = lax.axis_index("mem")
    up, down = lax.rem(grp + 1, groups), lax.rem(grp + groups - 1, groups)
    last = (mem == members - 1).astype(jnp.int32)
    first = (mem == 0).astype(jnp.int32)
    next_dev = (lax.rem(grp + last, groups), lax.rem(mem + 1, members))
    prev_dev = (lax.rem(grp + groups - first, groups), lax.rem(mem + members - 1, members))

    def p_copy(r):
        return pltpu.make_async_copy(p_hbm.at[pl.ds(KP * r, KP)], own.at[pl.ds(STRIDE * r + LEAD, KP)], p_sem)

    def a_copy(r):
        return pltpu.make_async_copy(a_hbm.at[pl.ds(KA * r, KA)], a_all.at[pl.ds(KA * r, KA)], a_sem.at[1])

    def early_copy(r, count):
        return pltpu.make_async_copy(
            a_hbm.at[pl.ds(KA * (HALO + r), KA * count)], a_early.at[pl.ds(KA * r, KA * count)], a_sem.at[0])

    def mid_copy(r, count):
        return pltpu.make_async_copy(
            a_hbm.at[pl.ds(KA * (HALO + EARLY + r), KA * count)], a_mid.at[pl.ds(KA * r, KA * count)], a_sem.at[2])

    whole_a = pltpu.make_async_copy(a_hbm, a_all.at[pl.ds(0, KA * cap)], a_sem.at[1])
    lax.fori_loop(0, cap, lambda r, _: (p_copy(r).start(), 0)[1], 0)
    lax.fori_loop(0, EARLY, lambda r, _: (early_copy(r, 1).start(), 0)[1], 0)
    lax.fori_loop(0, EARLY, lambda r, _: (mid_copy(r, 1).start(), 0)[1], 0)
    lax.fori_loop(0, cap, lambda r, _: (a_copy(r).start(), 0)[1], 0)

    barrier = pltpu.get_barrier_semaphore()

    def greet(step, _):
        pl.semaphore_signal(barrier, inc=1, device_id=(grp, lax.rem(mem + step, members)), device_id_type=MESH)
        return 0

    lax.fori_loop(1, members, greet, 0)
    for device in ((up, mem), (down, mem), next_dev, prev_dev):
        pl.semaphore_signal(barrier, inc=1, device_id=device, device_id_type=MESH)

    n = rows[grp, mem]
    ga = aggs[grp, mem]

    def fill_agg(r, carry):
        agg, rest = carry
        agg_tab[r] = agg
        rest = rest + ga
        step = (rest >= n).astype(jnp.int32)
        return jnp.minimum(agg + step, gmax), rest - step * n

    lax.fori_loop(0, cap + 1, fill_agg, (jnp.int32(0), jnp.int32(0)))

    def fill_start(a, carry):
        q, rest = carry
        start_tab[a] = jnp.where(a > ga, 2 * cap, q + (rest > 0).astype(jnp.int32))
        rest = rest + n
        for _ in range(LONG):
            step = (rest >= ga).astype(jnp.int32)
            q, rest = q + step, rest - step * ga
        return q, rest

    lax.fori_loop(0, gmax + 3, fill_start, (jnp.int32(0), jnp.int32(0)))


    def to_next(r):
        return pltpu.make_async_remote_copy(
            src_ref=ghost_out.at[pl.ds(KP * r, KP)], dst_ref=edge.at[pl.ds(STRIDE * r + LEAD, KP)],
            send_sem=halo_send.at[r], recv_sem=halo_recv.at[r], device_id=next_dev, device_id_type=MESH)

    def to_prev(r):
        return pltpu.make_async_remote_copy(
            src_ref=p_hbm.at[pl.ds(KP * r, KP)],
            dst_ref=edge.at[pl.ds(STRIDE * (5 * HALO + r) + LEAD, KP)],
            send_sem=halo_send.at[HALO + r], recv_sem=halo_recv.at[HALO + r],
            device_id=prev_dev, device_id_type=MESH)

    pl.semaphore_wait(barrier, members - 1 + 4)
    for r in range(HALO):
        to_prev(r).start()

    blank = jnp.zeros((tile, tile), BF16)

    def blank_row(table):
        def body(r, _):
            for e in range(LEAD):
                table[STRIDE * r + e] = blank
            return 0
        return body

    lax.fori_loop(0, cap + 1, blank_row(own), 0)
    lax.fori_loop(0, 6 * HALO + 1, blank_row(edge), 0)
    pt[cap] = jnp.zeros((KP * tile, tile), BF16)
    across, along = (lax.broadcasted_iota(jnp.int32, (tile, tile), axis) for axis in (0, 1))
    unit[...] = jnp.where(across == along, 1.0, 0.0).astype(BF16)
    a_early[KA * EARLY] = blank
    a_mid[KA * EARLY] = blank
    a_all[KA * cap] = blank

    def blank_band(s, _):
        band[s] = jnp.zeros((BAND, members, share, tile), F32)
        return 0

    lax.fori_loop(0, gmax + 2, blank_band, 0)

    whole = own.at[pl.ds(0, KP * cap)]
    pltpu.make_async_copy(whole, whole, p_sem).wait()
    for r in range(HALO):
        for q in range(KP):
            ghost_out[KP * r + q] = own[STRIDE * jnp.maximum(n - HALO + r, 0) + LEAD + q]
        to_next(r).start()

    def edge_table():
        for r in range(2 * HALO):
            for q in range(KP):
                edge[STRIDE * (HALO + r) + LEAD + q] = own[STRIDE * r + LEAD + q]
                edge[STRIDE * (3 * HALO + r) + LEAD + q] = own[STRIDE * jnp.maximum(n - 2 * HALO + r, 0) + LEAD + q]

    def ap_pair(position, row, a_ref, a_first, blank_tile, table, index_of):
        agg = agg_tab[row]
        begin, end, beyond = start_tab[agg], start_tab[agg + 1], start_tab[agg + 2]
        window = 2 * HALO + 2
        bases = []
        for w in range(window):
            target = row - HALO + w
            ahead = ((target >= end).astype(jnp.int32) + (target >= beyond).astype(jnp.int32)
                     - (target < begin).astype(jnp.int32))
            bases.append(STRIDE * index_of(target) + LEAD - 1 - ahead)

        def tile_at(line, offset):
            base = KA * (line - a_first)
            if offset == 0:
                return a_ref[base]
            index = jnp.int32(blank_tile)
            if abs(offset) <= HALO:
                for k in range(1, KA):
                    index = jnp.where(offs[k, line] == offset, base + k, index)
            return a_ref[index]

        lhs = jnp.concatenate(
            [jnp.concatenate([tile_at(row, w - HALO), tile_at(row + 1, w - HALO - 1)], axis=0)
             for w in range(window)], axis=1)
        same = agg_tab[row + 1] == agg
        lower = []
        for low, from_w in ((0, 0), (2, 0), (4, HALO)):
            rhs = jnp.concatenate(
                [jnp.concatenate([table[b + low], table[b + low + 1]], axis=1) for b in bases[from_w:]], axis=0)
            out = jnp.dot(lhs[:, from_w * tile:], rhs, preferred_element_type=F32)
            for e in (0, 1):
                if low + e < WIDE:
                    ap[position, low + e] = out[:tile, e * tile:(e + 1) * tile].astype(BF16)
                lower.append(out[tile:, e * tile:(e + 1) * tile])
        for e in range(WIDE):
            ap[position + 1, e] = jnp.where(same, lower[e], lower[e + 1]).astype(BF16)
        mine = [own[STRIDE * (row + t) + LEAD + q] for t in (0, 1) for q in range(KP)]
        turned = lax.dot_general(
            unit[...], jnp.concatenate(mine, axis=0), (((1,), (1,)), ((), ())), preferred_element_type=F32)
        for i in range(2 * KP):
            pt[position + i // KP, pl.ds(i % KP * tile, tile), :] = turned[:, i * tile:(i + 1) * tile].astype(BF16)

    def inner_index(target):
        return jnp.clip(target, 0, cap - 1)

    def edge_index(target):
        from_end = 5 * HALO + target - n
        index = jnp.where(jnp.logical_or(target >= n, target >= 2 * HALO), from_end, HALO + target)
        return jnp.clip(index, 0, 6 * HALO - 1)

    def place_of(row):
        place = jnp.where(row < HALO, inner + row, jnp.where(row >= n - HALO, cap - n + row, row - HALO))
        return jnp.clip(place, 0, cap - 1)

    def products(begin, end, put):
        left, right = [], []
        for t in range(LONG):
            live = begin + t < end
            place = place_of(begin + t)
            left.append(jnp.where(live, place, cap))
            right.append(jnp.where(live, place, 0))
        lhs = jnp.concatenate([pt[i] for i in left], axis=1)
        for low, high in ((0, 2), (2, 4), (4, 5)):
            rhs = jnp.concatenate(
                [jnp.concatenate([ap[i, e] for e in range(low, high)], axis=1) for i in right], axis=0)
            out = jnp.dot(lhs, rhs, preferred_element_type=F32)
            for e in range(low, high):
                for q in range(KP):
                    part = out[q * tile:(q + 1) * tile, (e - low) * tile:(e - low + 1) * tile]
                    put(q, e, part.reshape(members, share, tile))

    def aggregate(back):
        agg = back + ga - gmax
        begin = start_tab[jnp.maximum(agg, 0)]
        end = jnp.where(agg >= 1, start_tab[jnp.maximum(agg, 0) + 1], 0)

        def put(q, e, value):
            band[back + q, e - q + 2] += value

        products(begin, end, put)

    def pack(upper, lower):
        return jnp.concatenate([upper, lower], axis=1).astype(BF16)

    def piece(step, begin, size, index):
        away = lax.rem(step * 7, members)
        who = (lax.rem(mem // side + away // side, side) * side
               + lax.rem(lax.rem(mem, side) + lax.rem(away, side), side))
        return pltpu.make_async_remote_copy(
            src_ref=send.at[who, pl.ds(begin, size)], dst_ref=recv.at[mem, pl.ds(begin, size)],
            send_sem=send_sem.at[step - 1], recv_sem=recv_sem.at[index, step - 1],
            device_id=(grp, who), device_id_type=MESH)

    def kept(begin, size, index):
        return pltpu.make_async_copy(
            send.at[mem, pl.ds(begin, size)], recv.at[mem, pl.ds(begin, size)], self_sem.at[index])

    def send_out(begin, size, index):
        lax.fori_loop(1, members, lambda s, _: (piece(s, begin, size, index).start(), 0)[1], 0)
        kept(begin, size, index).start()

    def quarter(position, a_ref, a_first, blank_tile):
        for t in range(0, CHUNK, 2):
            ap_pair(position + t, HALO + position + t, a_ref, a_first, blank_tile, own, inner_index)

    def turn(w, a_ref, a_first, blank_tile):
        lax.fori_loop(
            0, 2, lambda h, _: (quarter(2 * CHUNK * w + CHUNK * h, a_ref, a_first, blank_tile), 0)[1], 0)
        aggregate(1 + 2 * w)
        aggregate(2 + 2 * w)

    def depart(w):
        for o in range(BAND):
            send[:, (w - 1) * BAND + o] = pack(band[1 + 2 * w, o], band[2 + 2 * w, o])
        send_out((w - 1) * BAND, BAND, w - 1)

    early_copy(0, EARLY).wait()
    turn(0, a_early, HALO, KA * EARLY)
    mid_copy(0, EARLY).wait()
    turn(1, a_mid, HALO + EARLY, KA * EARLY)
    depart(1)
    edge_table()
    whole_a.wait()

    def later(w, _):
        turn(w, a_all, 0, KA * cap)
        depart(w)
        return 0

    lax.fori_loop(2, inner // (2 * CHUNK), later, 0)

    for r in range(HALO):
        to_next(r).wait_recv()
        to_prev(r).wait_recv()

    def edge_rows(h, _):
        for t in range(0, CHUNK, 2):
            place = h * CHUNK + t
            row = jnp.where(place < HALO, place, jnp.maximum(n - 2 * HALO + place, 0))
            ap_pair(inner + place, row, a_all, 0, KA * cap, edge, edge_index)
        return 0

    lax.fori_loop(0, 2 * HALO // CHUNK, edge_rows, 0)
    aggregate(gmax - 1)

    def put_near(q, e, value):
        near[q, e] = value

    products(start_tab[0], start_tab[1], put_near)
    shift = jnp.clip(gmax - ga, 0, gmax - 1) + 1
    for o in range(BAND):
        upper, lower = band[shift, o], band[shift + 1, o]
        if 1 <= o <= WIDE:
            upper = upper + near[1, o - 1]
        if o < WIDE:
            lower = lower + near[2, o]
        send[:, (pairs - 2) * BAND + o] = pack(upper, lower)
    send_out((pairs - 2) * BAND, BAND, pairs - 2)
    for o in range(BAND):
        send[:, (pairs - 1) * BAND + o] = pack(band[gmax - 1, o], band[gmax, o])
    send_out((pairs - 1) * BAND, BAND, pairs - 1)
    for e in range(WIDE):
        send[:, spill + e] = pack(near[0, e], band[gmax + 1, e] + jnp.where(ga == 1, near[2, e], 0.0))
    send_out(spill, WIDE, pairs)

    def fill_row(c, carry):
        who, place = carry
        count = aggs[grp, who]
        slot = jnp.where(place < 2, gmax - 4 + place,
                         jnp.where(place >= count - 2, gmax + place - count, gmax - 2 + place - count))
        slot_tab[c] = jnp.clip(slot, 0, gmax - 1)
        who_tab[c] = who
        done = (place + 1 >= count).astype(jnp.int32)
        return jnp.minimum(who + done, members - 1), (1 - done) * (place + 1)

    lax.fori_loop(0, coarse, fill_row, (jnp.int32(0), jnp.int32(0)))

    def arrive(begin, size, index):
        lax.fori_loop(1, members, lambda s, _: (piece(s, begin, size, index).wait_recv(), 0)[1], 0)
        kept(begin, size, index).wait()

    def unpack(u, _):
        arrive(u * BAND, BAND, u)

        def body(who, _):
            for o in range(BAND):
                both = recv[who, u * BAND + o].astype(F32)
                band[2 * u, o, who] = both[:share]
                band[2 * u + 1, o, who] = both[share:]
            return 0

        return lax.fori_loop(0, members, body, 0)

    lax.fori_loop(0, pairs, unpack, 0)
    arrive(spill, WIDE, pairs)

    def unpack_spill(who, _):
        for e in range(WIDE):
            both = recv[who, spill + e].astype(F32)
            band[gmax, e + 2, who] = both[:share]
            band[gmax + 1, e, who] = both[share:]
        return 0

    lax.fori_loop(0, members, unpack_spill, 0)

    def add_spill(who, _):
        here, after = who, who + 1
        count = aggs[grp, who]
        for e in range(WIDE):
            band[gmax - 4, e, after] += band[gmax + 1, e, here]
            value = band[gmax, e + 2, after]
            band[gmax - 1, e + 2, here] += value
            band[gmax - 4, e + 2, here] += jnp.where(count == 1, value, 0.0)
            band[gmax - 3, e + 2, here] += jnp.where(count == 2, value, 0.0)
        return 0

    lax.fori_loop(0, members - 1, add_spill, 0)

    def coarse_row(row):
        row = jnp.clip(row, 0, coarse - 1)
        slot, who = slot_tab[row], who_tab[row]
        return [band[slot, o, who] for o in range(BAND)]

    def z_pack(h, _):
        for way, base in ((0, coarse - fmax), (1, 0)):
            one, two = coarse_row(base + 2 * h), coarse_row(base + 2 * h + 1)
            for o in range(BAND):
                zsend[way, h * BAND + o] = jnp.concatenate([one[o], two[o]], axis=0).astype(BF16)
        return 0

    lax.fori_loop(0, (fmax + 1) // 2, z_pack, 0)
    ways = [
        pltpu.make_async_remote_copy(
            src_ref=zsend.at[way], dst_ref=zrecv.at[way], send_sem=z_send.at[way], recv_sem=z_recv.at[way],
            device_id=(group, mem), device_id_type=MESH)
        for way, group in ((0, up), (1, down))
    ]
    for way in ways:
        way.start()

    take_lower = flows[0, down]
    take_upper = flows[1, up]
    give_back = flows[1, grp]
    middle = coarse - flows[0, grp] - give_back
    foreign[2 * fmax + 2] = jnp.zeros((BAND, share, tile), F32)

    def place(slot):
        return jnp.where(slot < take_lower, slot - take_lower,
                         jnp.where(slot < take_lower + middle, give_back + slot - take_lower,
                                   coarse + slot - take_lower - middle))

    def in_middle(slot):
        for o, value in enumerate(coarse_row(place(slot))):
            outv[slot, o] = value

    def at_end(slot):
        row = place(slot)
        live = slot < take_lower + middle + take_upper
        native = jnp.logical_and(live, jnp.logical_and(row >= 0, row < coarse))
        index = jnp.where(live, jnp.where(row < 0, fmax + row, fmax + 1 + row - coarse), 2 * fmax + 2)
        other = foreign[jnp.clip(index, 0, 2 * fmax + 2)]
        for o, value in enumerate(coarse_row(row)):
            outv[slot, o] = jnp.where(native, value, other[o])

    def gather_all(fill, begin, end):
        def body(h, _):
            for t in range(4):
                fill(jnp.minimum(begin + 4 * h + t, end - 1))
            return 0
        lax.fori_loop(0, (end - begin + 3) // 4, body, 0)

    tail = 1 + coarse - 2 * fmax
    gather_all(in_middle, fmax, tail)
    for way in ways:
        way.wait()

    def z_unpack(h, _):
        for way, base in ((0, 0), (1, fmax + 1)):
            for o in range(BAND):
                both = zrecv[way, h * BAND + o].astype(F32)
                foreign[base + 2 * h, o] = both[:share]
                foreign[base + 2 * h + 1, o] = both[share:]
        return 0

    lax.fori_loop(0, (fmax + 1) // 2, z_unpack, 0)
    for e in range(WIDE):
        foreign[fmax - 1, e + 2] += band[gmax, e + 2, 0]
        foreign[fmax + 1, e] += band[gmax + 1, e, members - 1]
    gather_all(at_end, 0, fmax)
    gather_all(at_end, tail, out_cap)
    lax.fori_loop(1, members, lambda s, _: (piece(s, 0, total, 0).wait_send(), 0)[1], 0)
    for r in range(HALO):
        to_next(r).wait_send()
        to_prev(r).wait_send()


def local(a_tiles, p_tiles, a_offsets, agg_counts, row_counts, flows):
    cap, _, tile, _ = a_tiles.shape
    groups, members = lax.axis_size("grp"), lax.axis_size("mem")
    gmax = cap // 4
    pairs = gmax // 2
    coarse = members * gmax // 2
    fmax = coarse // 8
    share = tile // members
    pieces = pairs * BAND + WIDE
    out_cap = coarse + 2 * fmax - 2
    handed = (fmax + 1) // 2 * BAND
    smem = pl.BlockSpec(memory_space=pltpu.SMEM)
    hbm = pl.BlockSpec(memory_space=pl.ANY)
    vmem = pl.BlockSpec(memory_space=pltpu.VMEM)
    return pl.pallas_call(
        functools.partial(fused, (groups, members, cap, tile)),
        out_shape=pltpu.VMEM((out_cap, BAND, share, tile), F32),
        in_specs=[hbm, hbm, smem, smem, smem, smem],
        out_specs=vmem,
        scratch_shapes=[
            pltpu.VMEM((KA * EARLY + 1, tile, tile), BF16),
            pltpu.VMEM((KA * EARLY + 1, tile, tile), BF16),
            pltpu.VMEM((KA * cap + 1, tile, tile), BF16),
            pltpu.VMEM((STRIDE * cap + LEAD, tile, tile), BF16),
            pltpu.VMEM((STRIDE * 6 * HALO + LEAD, tile, tile), BF16),
            pltpu.VMEM((HALO * KP, tile, tile), BF16),
            pltpu.VMEM((cap, WIDE, tile, tile), BF16),
            pltpu.VMEM((cap + 1, KP * tile, tile), BF16),
            pltpu.VMEM((tile, tile), BF16),
            pltpu.VMEM((gmax + 2, BAND, members, share, tile), F32),
            pltpu.VMEM((KP, WIDE, members, share, tile), F32),
            pltpu.VMEM((members, pieces, 2 * share, tile), BF16),
            pltpu.VMEM((members, pieces, 2 * share, tile), BF16),
            pltpu.VMEM((2 * fmax + 3, BAND, share, tile), F32),
            pltpu.VMEM((2, handed, 2 * share, tile), BF16),
            pltpu.VMEM((2, handed, 2 * share, tile), BF16),
            pltpu.SMEM((gmax + 3,), jnp.int32),
            pltpu.SMEM((cap + 1,), jnp.int32),
            pltpu.SMEM((coarse,), jnp.int32),
            pltpu.SMEM((coarse,), jnp.int32),
            pltpu.SemaphoreType.DMA((3,)),
            pltpu.SemaphoreType.DMA,
            pltpu.SemaphoreType.DMA((2 * HALO,)),
            pltpu.SemaphoreType.DMA((2 * HALO,)),
            pltpu.SemaphoreType.DMA((members - 1,)),
            pltpu.SemaphoreType.DMA((pairs + 1, members - 1)),
            pltpu.SemaphoreType.DMA((pairs + 1,)),
            pltpu.SemaphoreType.DMA((2,)),
            pltpu.SemaphoreType.DMA((2,)),
        ],
        compiler_params=pltpu.CompilerParams(
            collective_id=0, has_side_effects=True, vmem_limit_bytes=58 * 1024 * 1024),
        cost_estimate=pl.CostEstimate(flops=7_500_000_000, bytes_accessed=20_000_000, transcendentals=0),
    )(a_tiles.reshape(cap * KA, tile, tile), p_tiles.reshape(cap * KP, tile, tile), a_offsets.T,
      agg_counts, row_counts, flows.T)


def solution(mesh):
    placed = (
        P(("grp", "mem"), None, None, None),
        P(("grp", "mem"), None, None, None),
        P(("grp", "mem"), None),
        P(),
        P(),
        P(),
    )
    return jax.shard_map(
        local, mesh=mesh, in_specs=placed, out_specs=P("grp", None, "mem", None), check_vma=False
    )
```

```python
import functools

import jax
import jax.numpy as jnp
from jax import lax
from jax.experimental import pallas as pl
from jax.experimental.pallas import tpu as pltpu
from jax.sharding import PartitionSpec as P

MESH = pl.DeviceIdType.MESH
F32 = jnp.float32
BF16 = jnp.bfloat16
KA = 7
KP = 3
BAND = 7
HALO = 4
WIDE = 5
STRIDE = 6
LEAD = STRIDE - KP
CHUNK = 4
LONG = 8
EARLY = 8


def fused(sizes, a_hbm, p_hbm, offs, aggs, rows, flows, outv,
          a_early, a_mid, a_all, own, edge, ghost_out, ap, pt, band, near, send, recv, foreign, zsend, zrecv,
          start_tab, agg_tab, slot_tab, who_tab,
          a_sem, p_sem, halo_send, halo_recv, send_sem, recv_sem, self_sem, z_send, z_recv):
    groups, members, cap, tile = sizes
    gmax = cap // 4
    pairs = gmax // 2
    coarse = members * gmax // 2
    fmax = coarse // 8
    out_cap = outv.shape[0]
    share = tile // members
    side = 2 if members == 4 else 4
    spill = pairs * BAND - 1
    total = spill + WIDE
    fourth = (pairs - 2) * BAND
    fifth = fourth + BAND - 1
    inner = cap - 2 * HALO
    grp = lax.axis_index("grp")
    mem = lax.axis_index("mem")
    up, down = lax.rem(grp + 1, groups), lax.rem(grp + groups - 1, groups)
    last = (mem == members - 1).astype(jnp.int32)
    first = (mem == 0).astype(jnp.int32)
    next_dev = (lax.rem(grp + last, groups), lax.rem(mem + 1, members))
    prev_dev = (lax.rem(grp + groups - first, groups), lax.rem(mem + members - 1, members))

    barrier = pltpu.get_barrier_semaphore()

    def greet(step, _):
        pl.semaphore_signal(barrier, inc=1, device_id=(grp, lax.rem(mem + step, members)), device_id_type=MESH)
        return 0

    lax.fori_loop(1, members, greet, 0)
    for device in ((up, mem), (down, mem), next_dev, prev_dev):
        pl.semaphore_signal(barrier, inc=1, device_id=device, device_id_type=MESH)

    def p_copy(r):
        return pltpu.make_async_copy(p_hbm.at[pl.ds(KP * r, KP)], own.at[pl.ds(STRIDE * r + LEAD, KP)], p_sem)

    def a_copy(r):
        return pltpu.make_async_copy(a_hbm.at[pl.ds(KA * r, KA)], a_all.at[pl.ds(KA * r, KA)], a_sem.at[1])

    def early_copy(r, count):
        return pltpu.make_async_copy(
            a_hbm.at[pl.ds(KA * (HALO + r), KA * count)], a_early.at[pl.ds(KA * r, KA * count)], a_sem.at[0])

    def mid_copy(r, count):
        return pltpu.make_async_copy(
            a_hbm.at[pl.ds(KA * (HALO + EARLY + r), KA * count)], a_mid.at[pl.ds(KA * r, KA * count)], a_sem.at[2])

    whole_a = pltpu.make_async_copy(a_hbm, a_all.at[pl.ds(0, KA * cap)], a_sem.at[1])
    lax.fori_loop(0, cap, lambda r, _: (p_copy(r).start(), 0)[1], 0)

    n = rows[grp, mem]
    ga = aggs[grp, mem]


    def to_next(r):
        return pltpu.make_async_remote_copy(
            src_ref=ghost_out.at[pl.ds(KP * r, KP)], dst_ref=edge.at[pl.ds(STRIDE * r + LEAD, KP)],
            send_sem=halo_send.at[r], recv_sem=halo_recv.at[r], device_id=next_dev, device_id_type=MESH)

    def to_prev(r):
        return pltpu.make_async_remote_copy(
            src_ref=p_hbm.at[pl.ds(KP * r, KP)],
            dst_ref=edge.at[pl.ds(STRIDE * (5 * HALO + r) + LEAD, KP)],
            send_sem=halo_send.at[HALO + r], recv_sem=halo_recv.at[HALO + r],
            device_id=prev_dev, device_id_type=MESH)

    pl.semaphore_wait(barrier, members - 1 + 4)
    for r in range(HALO):
        to_prev(r).start()
    lax.fori_loop(0, EARLY, lambda r, _: (early_copy(r, 1).start(), 0)[1], 0)
    lax.fori_loop(0, EARLY, lambda r, _: (mid_copy(r, 1).start(), 0)[1], 0)
    lax.fori_loop(0, cap, lambda r, _: (a_copy(r).start(), 0)[1], 0)

    blank = jnp.zeros((tile, tile), BF16)

    def blank_row(table):
        def body(r, _):
            for e in range(LEAD):
                table[STRIDE * r + e] = blank
            return 0
        return body

    lax.fori_loop(0, cap + 1, blank_row(own), 0)
    lax.fori_loop(0, 6 * HALO + 1, blank_row(edge), 0)
    pt[cap] = jnp.zeros((KP * tile, tile), BF16)
    a_early[KA * EARLY] = blank
    a_mid[KA * EARLY] = blank
    a_all[KA * cap] = blank

    def blank_band(s, _):
        band[s] = jnp.zeros((BAND, members, share, tile), F32)
        return 0

    lax.fori_loop(0, gmax + 2, blank_band, 0)

    whole = own.at[pl.ds(0, KP * cap)]
    pltpu.make_async_copy(whole, whole, p_sem).wait()
    for r in range(HALO):
        for q in range(KP):
            ghost_out[KP * r + q] = own[STRIDE * jnp.maximum(n - HALO + r, 0) + LEAD + q]
        to_next(r).start()

    def edge_table():
        for r in range(2 * HALO):
            for q in range(KP):
                edge[STRIDE * (HALO + r) + LEAD + q] = own[STRIDE * r + LEAD + q]
                edge[STRIDE * (3 * HALO + r) + LEAD + q] = own[STRIDE * jnp.maximum(n - 2 * HALO + r, 0) + LEAD + q]

    def fill_agg(r, carry):
        agg, rest = carry
        agg_tab[r] = agg
        rest = rest + ga
        step = (rest >= n).astype(jnp.int32)
        return jnp.minimum(agg + step, gmax), rest - step * n

    lax.fori_loop(0, cap + 1, fill_agg, (jnp.int32(0), jnp.int32(0)))

    def fill_start(a, carry):
        q, rest = carry
        start_tab[a] = jnp.where(a > ga, 2 * cap, q + (rest > 0).astype(jnp.int32))
        rest = rest + n
        for _ in range(LONG):
            step = (rest >= ga).astype(jnp.int32)
            q, rest = q + step, rest - step * ga
        return q, rest

    lax.fori_loop(0, gmax + 3, fill_start, (jnp.int32(0), jnp.int32(0)))

    def ap_pair(position, row, a_ref, a_first, blank_tile, table, index_of):
        agg = agg_tab[row]
        begin, end, beyond = start_tab[agg], start_tab[agg + 1], start_tab[agg + 2]
        window = 2 * HALO + 2
        bases = []
        for w in range(window):
            target = row - HALO + w
            ahead = ((target >= end).astype(jnp.int32) + (target >= beyond).astype(jnp.int32)
                     - (target < begin).astype(jnp.int32))
            bases.append(STRIDE * index_of(target) + LEAD - 1 - ahead)

        def tile_at(line, offset):
            base = KA * (line - a_first)
            if offset == 0:
                return a_ref[base]
            index = jnp.int32(blank_tile)
            if abs(offset) <= HALO:
                for k in range(1, KA):
                    index = jnp.where(offs[k, line] == offset, base + k, index)
            return a_ref[index]

        lhs = jnp.concatenate(
            [jnp.concatenate([tile_at(row, w - HALO), tile_at(row + 1, w - HALO - 1)], axis=0)
             for w in range(window)], axis=1)
        same = agg_tab[row + 1] == agg
        lower = []
        for low, from_w in ((0, 0), (2, 0), (4, HALO)):
            rhs = jnp.concatenate(
                [jnp.concatenate([table[b + low], table[b + low + 1]], axis=1) for b in bases[from_w:]], axis=0)
            out = jnp.dot(lhs[:, from_w * tile:], rhs, preferred_element_type=F32)
            for e in (0, 1):
                if low + e < WIDE:
                    ap[position, low + e] = out[:tile, e * tile:(e + 1) * tile].astype(BF16)
                lower.append(out[tile:, e * tile:(e + 1) * tile])
        for e in range(WIDE):
            ap[position + 1, e] = jnp.where(same, lower[e], lower[e + 1]).astype(BF16)
        for t in (0, 1):
            for q in range(KP):
                pt[position + t, pl.ds(q * tile, tile), :] = own[STRIDE * (row + t) + LEAD + q].T

    def inner_index(target):
        return jnp.clip(target, 0, cap - 1)

    def edge_index(target):
        from_end = 5 * HALO + target - n
        index = jnp.where(jnp.logical_or(target >= n, target >= 2 * HALO), from_end, HALO + target)
        return jnp.clip(index, 0, 6 * HALO - 1)

    def place_of(row):
        place = jnp.where(row < HALO, inner + row, jnp.where(row >= n - HALO, cap - n + row, row - HALO))
        return jnp.clip(place, 0, cap - 1)

    def products(begin, end, put):
        left, right = [], []
        for t in range(LONG):
            live = begin + t < end
            place = place_of(begin + t)
            left.append(jnp.where(live, place, cap))
            right.append(jnp.where(live, place, 0))
        lhs = jnp.concatenate([pt[i] for i in left], axis=1)
        for low, high in ((0, 2), (2, 4), (4, 5)):
            rhs = jnp.concatenate(
                [jnp.concatenate([ap[i, e] for e in range(low, high)], axis=1) for i in right], axis=0)
            out = jnp.dot(lhs, rhs, preferred_element_type=F32)
            for e in range(low, high):
                for q in range(KP):
                    part = out[q * tile:(q + 1) * tile, (e - low) * tile:(e - low + 1) * tile]
                    put(q, e, part.reshape(members, share, tile))

    def aggregate(back):
        agg = back + ga - gmax
        begin = start_tab[jnp.maximum(agg, 0)]
        end = jnp.where(agg >= 1, start_tab[jnp.maximum(agg, 0) + 1], 0)

        def put(q, e, value):
            band[back + q, e - q + 2] += value

        products(begin, end, put)

    def pack(upper, lower):
        return jnp.concatenate([upper, lower], axis=1).astype(BF16)

    def piece(step, begin, size, index):
        away = lax.rem(step * 7, members)
        who = (lax.rem(mem // side + away // side, side) * side
               + lax.rem(lax.rem(mem, side) + lax.rem(away, side), side))
        return pltpu.make_async_remote_copy(
            src_ref=send.at[who, pl.ds(begin, size)], dst_ref=recv.at[mem, pl.ds(begin, size)],
            send_sem=send_sem.at[step - 1], recv_sem=recv_sem.at[index, step - 1],
            device_id=(grp, who), device_id_type=MESH)

    def kept(begin, size, index):
        return pltpu.make_async_copy(
            send.at[mem, pl.ds(begin, size)], recv.at[mem, pl.ds(begin, size)], self_sem.at[index])

    def send_out(begin, size, index):
        lax.fori_loop(1, members, lambda s, _: (piece(s, begin, size, index).start(), 0)[1], 0)
        kept(begin, size, index).start()

    def quarter(position, a_ref, a_first, blank_tile):
        for t in range(0, CHUNK, 2):
            ap_pair(position + t, HALO + position + t, a_ref, a_first, blank_tile, own, inner_index)

    def turn(w, a_ref, a_first, blank_tile):
        lax.fori_loop(
            0, 2, lambda h, _: (quarter(2 * CHUNK * w + CHUNK * h, a_ref, a_first, blank_tile), 0)[1], 0)
        aggregate(1 + 2 * w)
        aggregate(2 + 2 * w)

    def depart(w):
        for o in range(BAND):
            send[:, (w - 1) * BAND + o] = pack(band[1 + 2 * w, o], band[2 + 2 * w, o])
        send_out((w - 1) * BAND, BAND, w - 1)

    early_copy(0, EARLY).wait()
    turn(0, a_early, HALO, KA * EARLY)
    mid_copy(0, EARLY).wait()
    turn(1, a_mid, HALO + EARLY, KA * EARLY)
    depart(1)
    edge_table()
    whole_a.wait()

    def later(w, _):
        turn(w, a_all, 0, KA * cap)
        depart(w)
        return 0

    lax.fori_loop(2, inner // (2 * CHUNK), later, 0)

    for r in range(HALO):
        to_next(r).wait_recv()
        to_prev(r).wait_recv()

    def edge_rows(h, _):
        for t in range(0, CHUNK, 2):
            place = h * CHUNK + t
            row = jnp.where(place < HALO, place, jnp.maximum(n - 2 * HALO + place, 0))
            ap_pair(inner + place, row, a_all, 0, KA * cap, edge, edge_index)
        return 0

    lax.fori_loop(0, 2 * HALO // CHUNK, edge_rows, 0)
    aggregate(gmax - 1)

    def put_near(q, e, value):
        near[q, e] = value

    products(start_tab[0], start_tab[1], put_near)
    shift = jnp.clip(gmax - ga, 0, gmax - 1) + 1
    for o in range(BAND):
        lower = band[shift + 1, o]
        if o < WIDE:
            lower = lower + near[2, o]
        if o == 0:
            send[:, spill - 1] = pack(band[gmax - 1, BAND - 1], lower)
            continue
        upper = band[shift, o]
        if o <= WIDE:
            upper = upper + near[1, o - 1]
        send[:, fourth + o - 1] = pack(upper, lower)
    send_out(fourth, BAND - 1, pairs - 2)
    for o in range(BAND - 1):
        send[:, fifth + o] = pack(band[gmax - 1, o], band[gmax, o])
    send_out(fifth, BAND, pairs - 1)
    for e in range(WIDE):
        send[:, spill + e] = pack(near[0, e], band[gmax + 1, e] + jnp.where(ga == 1, near[2, e], 0.0))
    send_out(spill, WIDE, pairs)

    def fill_row(c, carry):
        who, place = carry
        count = aggs[grp, who]
        slot = jnp.where(place < 2, gmax - 4 + place,
                         jnp.where(place >= count - 2, gmax + place - count, gmax - 2 + place - count))
        slot_tab[c] = jnp.clip(slot, 0, gmax - 1)
        who_tab[c] = who
        done = (place + 1 >= count).astype(jnp.int32)
        return jnp.minimum(who + done, members - 1), (1 - done) * (place + 1)

    lax.fori_loop(0, coarse, fill_row, (jnp.int32(0), jnp.int32(0)))

    def arrive(begin, size, index):
        lax.fori_loop(1, members, lambda s, _: (piece(s, begin, size, index).wait_recv(), 0)[1], 0)
        kept(begin, size, index).wait()

    def unpack(u, _):
        arrive(u * BAND, BAND, u)

        def body(who, _):
            for o in range(BAND):
                both = recv[who, u * BAND + o].astype(F32)
                band[2 * u, o, who] = both[:share]
                band[2 * u + 1, o, who] = both[share:]
            return 0

        return lax.fori_loop(0, members, body, 0)

    lax.fori_loop(0, pairs - 2, unpack, 0)
    nothing = jnp.zeros((share, tile), F32)
    arrive(fourth, BAND - 1, pairs - 2)

    def unpack_fourth(who, _):
        band[gmax - 4, 0, who] = nothing
        for o in range(1, BAND):
            both = recv[who, fourth + o - 1].astype(F32)
            band[gmax - 4, o, who] = both[:share]
            band[gmax - 3, o, who] = both[share:]
        return 0

    lax.fori_loop(0, members, unpack_fourth, 0)
    arrive(fifth, BAND, pairs - 1)

    def unpack_fifth(who, _):
        for o in range(BAND - 1):
            both = recv[who, fifth + o].astype(F32)
            band[gmax - 2, o, who] = both[:share]
            band[gmax - 1, o, who] = both[share:]
        both = recv[who, spill - 1].astype(F32)
        band[gmax - 2, BAND - 1, who] = both[:share]
        band[gmax - 1, BAND - 1, who] = nothing
        band[gmax - 3, 0, who] = both[share:]
        return 0

    lax.fori_loop(0, members, unpack_fifth, 0)
    arrive(spill, WIDE, pairs)

    def unpack_spill(who, _):
        for e in range(WIDE):
            both = recv[who, spill + e].astype(F32)
            band[gmax, e + 2, who] = both[:share]
            band[gmax + 1, e, who] = both[share:]
        return 0

    lax.fori_loop(0, members, unpack_spill, 0)

    def add_spill(who, _):
        here, after = who, who + 1
        count = aggs[grp, who]
        for e in range(WIDE):
            band[gmax - 4, e, after] += band[gmax + 1, e, here]
            value = band[gmax, e + 2, after]
            band[gmax - 1, e + 2, here] += value
            band[gmax - 4, e + 2, here] += jnp.where(count == 1, value, 0.0)
            band[gmax - 3, e + 2, here] += jnp.where(count == 2, value, 0.0)
        return 0

    lax.fori_loop(0, members - 1, add_spill, 0)

    def coarse_row(row):
        row = jnp.clip(row, 0, coarse - 1)
        slot, who = slot_tab[row], who_tab[row]
        return [band[slot, o, who] for o in range(BAND)]

    def z_pack(way, base):
        def body(h, _):
            one, two = coarse_row(base + 2 * h), coarse_row(base + 2 * h + 1)
            for o in range(BAND):
                zsend[way, h * BAND + o] = jnp.concatenate([one[o], two[o]], axis=0).astype(BF16)
            return 0
        lax.fori_loop(0, (fmax + 1) // 2, body, 0)

    ways = [
        pltpu.make_async_remote_copy(
            src_ref=zsend.at[way], dst_ref=zrecv.at[way], send_sem=z_send.at[way], recv_sem=z_recv.at[way],
            device_id=(group, mem), device_id_type=MESH)
        for way, group in ((0, up), (1, down))
    ]
    z_pack(0, coarse - fmax)
    ways[0].start()
    z_pack(1, 0)
    ways[1].start()

    take_lower = flows[0, down]
    take_upper = flows[1, up]
    give_back = flows[1, grp]
    middle = coarse - flows[0, grp] - give_back
    foreign[2 * fmax + 2] = jnp.zeros((BAND, share, tile), F32)

    def place(slot):
        return jnp.where(slot < take_lower, slot - take_lower,
                         jnp.where(slot < take_lower + middle, give_back + slot - take_lower,
                                   coarse + slot - take_lower - middle))

    def in_middle(slot):
        for o, value in enumerate(coarse_row(place(slot))):
            outv[slot, o] = value

    def at_end(slot):
        row = place(slot)
        live = slot < take_lower + middle + take_upper
        native = jnp.logical_and(live, jnp.logical_and(row >= 0, row < coarse))
        index = jnp.where(live, jnp.where(row < 0, fmax + row, fmax + 1 + row - coarse), 2 * fmax + 2)
        other = foreign[jnp.clip(index, 0, 2 * fmax + 2)]
        for o, value in enumerate(coarse_row(row)):
            outv[slot, o] = jnp.where(native, value, other[o])

    def gather_all(fill, begin, end):
        def body(h, _):
            for t in range(4):
                fill(jnp.minimum(begin + 4 * h + t, end - 1))
            return 0
        lax.fori_loop(0, (end - begin + 3) // 4, body, 0)

    tail = 1 + coarse - 2 * fmax
    gather_all(in_middle, fmax, tail)

    def z_unpack(way, base):
        def body(h, _):
            for o in range(BAND):
                both = zrecv[way, h * BAND + o].astype(F32)
                foreign[base + 2 * h, o] = both[:share]
                foreign[base + 2 * h + 1, o] = both[share:]
            return 0
        lax.fori_loop(0, (fmax + 1) // 2, body, 0)

    for way in ways:
        way.wait_recv()
    z_unpack(0, 0)
    z_unpack(1, fmax + 1)
    for e in range(WIDE):
        foreign[fmax - 1, e + 2] += band[gmax, e + 2, 0]
        foreign[fmax + 1, e] += band[gmax + 1, e, members - 1]
    gather_all(at_end, 0, fmax)
    gather_all(at_end, tail, out_cap)
    for way in ways:
        way.wait_send()
    lax.fori_loop(1, members, lambda s, _: (piece(s, 0, total, 0).wait_send(), 0)[1], 0)
    for r in range(HALO):
        to_next(r).wait_send()
        to_prev(r).wait_send()


def local(a_tiles, p_tiles, a_offsets, agg_counts, row_counts, flows):
    cap, _, tile, _ = a_tiles.shape
    groups, members = lax.axis_size("grp"), lax.axis_size("mem")
    gmax = cap // 4
    pairs = gmax // 2
    coarse = members * gmax // 2
    fmax = coarse // 8
    share = tile // members
    pieces = pairs * BAND - 1 + WIDE
    out_cap = coarse + 2 * fmax - 2
    handed = (fmax + 1) // 2 * BAND
    smem = pl.BlockSpec(memory_space=pltpu.SMEM)
    hbm = pl.BlockSpec(memory_space=pl.ANY)
    vmem = pl.BlockSpec(memory_space=pltpu.VMEM)
    return pl.pallas_call(
        functools.partial(fused, (groups, members, cap, tile)),
        out_shape=pltpu.VMEM((out_cap, BAND, share, tile), F32),
        in_specs=[hbm, hbm, smem, smem, smem, smem],
        out_specs=vmem,
        scratch_shapes=[
            pltpu.VMEM((KA * EARLY + 1, tile, tile), BF16),
            pltpu.VMEM((KA * EARLY + 1, tile, tile), BF16),
            pltpu.VMEM((KA * cap + 1, tile, tile), BF16),
            pltpu.VMEM((STRIDE * cap + LEAD, tile, tile), BF16),
            pltpu.VMEM((STRIDE * 6 * HALO + LEAD, tile, tile), BF16),
            pltpu.VMEM((HALO * KP, tile, tile), BF16),
            pltpu.VMEM((cap, WIDE, tile, tile), BF16),
            pltpu.VMEM((cap + 1, KP * tile, tile), BF16),
            pltpu.VMEM((gmax + 2, BAND, members, share, tile), F32),
            pltpu.VMEM((KP, WIDE, members, share, tile), F32),
            pltpu.VMEM((members, pieces, 2 * share, tile), BF16),
            pltpu.VMEM((members, pieces, 2 * share, tile), BF16),
            pltpu.VMEM((2 * fmax + 3, BAND, share, tile), F32),
            pltpu.VMEM((2, handed, 2 * share, tile), BF16),
            pltpu.VMEM((2, handed, 2 * share, tile), BF16),
            pltpu.SMEM((gmax + 3,), jnp.int32),
            pltpu.SMEM((cap + 1,), jnp.int32),
            pltpu.SMEM((coarse,), jnp.int32),
            pltpu.SMEM((coarse,), jnp.int32),
            pltpu.SemaphoreType.DMA((3,)),
            pltpu.SemaphoreType.DMA,
            pltpu.SemaphoreType.DMA((2 * HALO,)),
            pltpu.SemaphoreType.DMA((2 * HALO,)),
            pltpu.SemaphoreType.DMA((members - 1,)),
            pltpu.SemaphoreType.DMA((pairs + 1, members - 1)),
            pltpu.SemaphoreType.DMA((pairs + 1,)),
            pltpu.SemaphoreType.DMA((2,)),
            pltpu.SemaphoreType.DMA((2,)),
        ],
        compiler_params=pltpu.CompilerParams(
            collective_id=0, has_side_effects=True, vmem_limit_bytes=58 * 1024 * 1024),
        cost_estimate=pl.CostEstimate(flops=7_500_000_000, bytes_accessed=20_000_000, transcendentals=0),
    )(a_tiles.reshape(cap * KA, tile, tile), p_tiles.reshape(cap * KP, tile, tile), a_offsets.T,
      agg_counts, row_counts, flows.T)


def solution(mesh):
    placed = (
        P(("grp", "mem"), None, None, None),
        P(("grp", "mem"), None, None, None),
        P(("grp", "mem"), None),
        P(),
        P(),
        P(),
    )
    return jax.shard_map(
        local, mesh=mesh, in_specs=placed, out_specs=P("grp", None, "mem", None), check_vma=False
    )
```

```python
import functools

import jax
import jax.numpy as jnp
from jax import lax
from jax.experimental import pallas as pl
from jax.experimental.pallas import tpu as pltpu
from jax.sharding import PartitionSpec as P

MESH = pl.DeviceIdType.MESH
F32 = jnp.float32
BF16 = jnp.bfloat16
KA = 7
KP = 3
BAND = 7
HALO = 4
WIDE = 5
STRIDE = 6
LEAD = STRIDE - KP
CHUNK = 4
LONG = 8
EARLY = 8


def fused(sizes, a_hbm, p_hbm, offs, aggs, rows, flows, outv,
          a_early, a_mid, a_all, own, edge, ghost_out, ap, pt, band, near, send, recv, foreign, zsend, zrecv,
          start_tab, agg_tab, slot_tab, who_tab,
          a_sem, p_sem, halo_send, halo_recv, send_sem, recv_sem, self_sem, z_send, z_recv):
    groups, members, cap, tile = sizes
    gmax = cap // 4
    pairs = gmax // 2
    coarse = members * gmax // 2
    fmax = coarse // 8
    out_cap = outv.shape[0]
    share = tile // members
    side = 2 if members == 4 else 4
    spill = pairs * BAND - 1
    total = spill + WIDE
    fourth = (pairs - 2) * BAND
    fifth = fourth + BAND - 1
    inner = cap - 2 * HALO
    grp = lax.axis_index("grp")
    mem = lax.axis_index("mem")
    up, down = lax.rem(grp + 1, groups), lax.rem(grp + groups - 1, groups)
    last = (mem == members - 1).astype(jnp.int32)
    first = (mem == 0).astype(jnp.int32)
    next_dev = (lax.rem(grp + last, groups), lax.rem(mem + 1, members))
    prev_dev = (lax.rem(grp + groups - first, groups), lax.rem(mem + members - 1, members))

    barrier = pltpu.get_barrier_semaphore()

    def greet(step, _):
        pl.semaphore_signal(barrier, inc=1, device_id=(grp, lax.rem(mem + step, members)), device_id_type=MESH)
        return 0

    lax.fori_loop(1, members, greet, 0)
    for device in ((up, mem), (down, mem), next_dev, prev_dev):
        pl.semaphore_signal(barrier, inc=1, device_id=device, device_id_type=MESH)

    def p_copy(r):
        return pltpu.make_async_copy(p_hbm.at[pl.ds(KP * r, KP)], own.at[pl.ds(STRIDE * r + LEAD, KP)], p_sem)

    def a_copy(r):
        return pltpu.make_async_copy(a_hbm.at[pl.ds(KA * r, KA)], a_all.at[pl.ds(KA * r, KA)], a_sem.at[1])

    def early_copy(r, count):
        return pltpu.make_async_copy(
            a_hbm.at[pl.ds(KA * (HALO + r), KA * count)], a_early.at[pl.ds(KA * r, KA * count)], a_sem.at[0])

    def mid_copy(r, count):
        return pltpu.make_async_copy(
            a_hbm.at[pl.ds(KA * (HALO + EARLY + r), KA * count)], a_mid.at[pl.ds(KA * r, KA * count)], a_sem.at[2])

    whole_a = pltpu.make_async_copy(a_hbm, a_all.at[pl.ds(0, KA * cap)], a_sem.at[1])
    lax.fori_loop(0, cap, lambda r, _: (p_copy(r).start(), 0)[1], 0)

    n = rows[grp, mem]
    ga = aggs[grp, mem]


    def to_next(r):
        return pltpu.make_async_remote_copy(
            src_ref=ghost_out.at[pl.ds(KP * r, KP)], dst_ref=edge.at[pl.ds(STRIDE * r + LEAD, KP)],
            send_sem=halo_send.at[r], recv_sem=halo_recv.at[r], device_id=next_dev, device_id_type=MESH)

    def to_prev(r):
        return pltpu.make_async_remote_copy(
            src_ref=p_hbm.at[pl.ds(KP * r, KP)],
            dst_ref=edge.at[pl.ds(STRIDE * (5 * HALO + r) + LEAD, KP)],
            send_sem=halo_send.at[HALO + r], recv_sem=halo_recv.at[HALO + r],
            device_id=prev_dev, device_id_type=MESH)

    pl.semaphore_wait(barrier, members - 1 + 4)
    for r in range(HALO):
        to_prev(r).start()
    lax.fori_loop(0, EARLY, lambda r, _: (early_copy(r, 1).start(), 0)[1], 0)
    lax.fori_loop(0, EARLY, lambda r, _: (mid_copy(r, 1).start(), 0)[1], 0)
    lax.fori_loop(0, cap, lambda r, _: (a_copy(r).start(), 0)[1], 0)

    blank = jnp.zeros((tile, tile), BF16)

    def blank_row(table):
        def body(r, _):
            for e in range(LEAD):
                table[STRIDE * r + e] = blank
            return 0
        return body

    lax.fori_loop(0, cap + 1, blank_row(own), 0)
    lax.fori_loop(0, 6 * HALO + 1, blank_row(edge), 0)
    pt[cap] = jnp.zeros((KP * tile, tile), BF16)
    a_early[KA * EARLY] = blank
    a_mid[KA * EARLY] = blank
    a_all[KA * cap] = blank

    def blank_band(s, _):
        band[s] = jnp.zeros((BAND, members, share, tile), F32)
        return 0

    lax.fori_loop(0, gmax + 2, blank_band, 0)

    whole = own.at[pl.ds(0, KP * cap)]
    pltpu.make_async_copy(whole, whole, p_sem).wait()
    for r in range(HALO):
        for q in range(KP):
            ghost_out[KP * r + q] = own[STRIDE * jnp.maximum(n - HALO + r, 0) + LEAD + q]
        to_next(r).start()

    def edge_table():
        for r in range(2 * HALO):
            for q in range(KP):
                edge[STRIDE * (HALO + r) + LEAD + q] = own[STRIDE * r + LEAD + q]
                edge[STRIDE * (3 * HALO + r) + LEAD + q] = own[STRIDE * jnp.maximum(n - 2 * HALO + r, 0) + LEAD + q]

    def fill_agg(r, carry):
        agg, rest = carry
        agg_tab[r] = agg
        rest = rest + ga
        step = (rest >= n).astype(jnp.int32)
        return jnp.minimum(agg + step, gmax), rest - step * n

    lax.fori_loop(0, cap + 1, fill_agg, (jnp.int32(0), jnp.int32(0)))

    def fill_start(a, carry):
        q, rest = carry
        start_tab[a] = jnp.where(a > ga, 2 * cap, q + (rest > 0).astype(jnp.int32))
        rest = rest + n
        for _ in range(LONG):
            step = (rest >= ga).astype(jnp.int32)
            q, rest = q + step, rest - step * ga
        return q, rest

    lax.fori_loop(0, gmax + 3, fill_start, (jnp.int32(0), jnp.int32(0)))

    def ap_pair(position, row, a_ref, a_first, blank_tile, table, index_of):
        agg = agg_tab[row]
        begin, end, beyond = start_tab[agg], start_tab[agg + 1], start_tab[agg + 2]
        window = 2 * HALO + 2
        bases = []
        for w in range(window):
            target = row - HALO + w
            ahead = ((target >= end).astype(jnp.int32) + (target >= beyond).astype(jnp.int32)
                     - (target < begin).astype(jnp.int32))
            bases.append(STRIDE * index_of(target) + LEAD - 1 - ahead)

        def tile_at(line, offset):
            base = KA * (line - a_first)
            if offset == 0:
                return a_ref[base]
            index = jnp.int32(blank_tile)
            if abs(offset) <= HALO:
                for k in range(1, KA):
                    index = jnp.where(offs[k, line] == offset, base + k, index)
            return a_ref[index]

        lhs = jnp.concatenate(
            [jnp.concatenate([tile_at(row, w - HALO), tile_at(row + 1, w - HALO - 1)], axis=0)
             for w in range(window)], axis=1)
        same = agg_tab[row + 1] == agg
        lower = []
        for low, from_w in ((0, 0), (2, 0), (4, HALO)):
            rhs = jnp.concatenate(
                [jnp.concatenate([table[b + low], table[b + low + 1]], axis=1) for b in bases[from_w:]], axis=0)
            out = jnp.dot(lhs[:, from_w * tile:], rhs, preferred_element_type=F32)
            for e in (0, 1):
                if low + e < WIDE:
                    ap[position, low + e] = out[:tile, e * tile:(e + 1) * tile].astype(BF16)
                lower.append(out[tile:, e * tile:(e + 1) * tile])
        for e in range(WIDE):
            ap[position + 1, e] = jnp.where(same, lower[e], lower[e + 1]).astype(BF16)
        for t in (0, 1):
            for q in range(KP):
                pt[position + t, pl.ds(q * tile, tile), :] = own[STRIDE * (row + t) + LEAD + q].T

    def inner_index(target):
        return jnp.clip(target, 0, cap - 1)

    def edge_index(target):
        from_end = 5 * HALO + target - n
        index = jnp.where(jnp.logical_or(target >= n, target >= 2 * HALO), from_end, HALO + target)
        return jnp.clip(index, 0, 6 * HALO - 1)

    def place_of(row):
        place = jnp.where(row < HALO, inner + row, jnp.where(row >= n - HALO, cap - n + row, row - HALO))
        return jnp.clip(place, 0, cap - 1)

    def products(begin, end, put):
        left, right = [], []
        for t in range(LONG):
            live = begin + t < end
            place = place_of(begin + t)
            left.append(jnp.where(live, place, cap))
            right.append(jnp.where(live, place, 0))
        lhs = jnp.concatenate([pt[i] for i in left], axis=1)
        for low, high in ((0, 2), (2, 4), (4, 5)):
            rhs = jnp.concatenate(
                [jnp.concatenate([ap[i, e] for e in range(low, high)], axis=1) for i in right], axis=0)
            out = jnp.dot(lhs, rhs, preferred_element_type=F32)
            for e in range(low, high):
                for q in range(KP):
                    part = out[q * tile:(q + 1) * tile, (e - low) * tile:(e - low + 1) * tile]
                    put(q, e, part.reshape(members, share, tile))

    def aggregate(back):
        agg = back + ga - gmax
        begin = start_tab[jnp.maximum(agg, 0)]
        end = jnp.where(agg >= 1, start_tab[jnp.maximum(agg, 0) + 1], 0)

        def put(q, e, value):
            band[back + q, e - q + 2] += value

        products(begin, end, put)

    def pack(upper, lower):
        return jnp.concatenate([upper, lower], axis=1).astype(BF16)

    def piece(step, begin, size, index):
        away = lax.rem(step * 7, members)
        who = (lax.rem(mem // side + away // side, side) * side
               + lax.rem(lax.rem(mem, side) + lax.rem(away, side), side))
        return pltpu.make_async_remote_copy(
            src_ref=send.at[who, pl.ds(begin, size)], dst_ref=recv.at[mem, pl.ds(begin, size)],
            send_sem=send_sem.at[step - 1], recv_sem=recv_sem.at[index, step - 1],
            device_id=(grp, who), device_id_type=MESH)

    def kept(begin, size, index):
        return pltpu.make_async_copy(
            send.at[mem, pl.ds(begin, size)], recv.at[mem, pl.ds(begin, size)], self_sem.at[index])

    def send_out(begin, size, index):
        lax.fori_loop(1, members, lambda s, _: (piece(s, begin, size, index).start(), 0)[1], 0)
        kept(begin, size, index).start()

    def quarter(position, a_ref, a_first, blank_tile):
        for t in range(0, CHUNK, 2):
            ap_pair(position + t, HALO + position + t, a_ref, a_first, blank_tile, own, inner_index)

    def turn(w, a_ref, a_first, blank_tile):
        lax.fori_loop(
            0, 2, lambda h, _: (quarter(2 * CHUNK * w + CHUNK * h, a_ref, a_first, blank_tile), 0)[1], 0)
        aggregate(1 + 2 * w)
        aggregate(2 + 2 * w)

    def depart(w):
        for o in range(BAND):
            send[:, (w - 1) * BAND + o] = pack(band[1 + 2 * w, o], band[2 + 2 * w, o])

    early_copy(0, EARLY).wait()
    turn(0, a_early, HALO, KA * EARLY)
    mid_copy(0, EARLY).wait()
    turn(1, a_mid, HALO + EARLY, KA * EARLY)
    depart(1)
    send_out(0, BAND, 0)
    edge_table()
    whole_a.wait()

    def later(w, _):
        turn(w, a_all, 0, KA * cap)
        depart(w)

        @pl.when(w == 2)
        def _():
            send_out(BAND, BAND, 1)

        return 0

    lax.fori_loop(2, inner // (2 * CHUNK), later, 0)
    send_out(2 * BAND, fourth - 2 * BAND, 2)

    for r in range(HALO):
        to_next(r).wait_recv()
        to_prev(r).wait_recv()

    def edge_rows(h, _):
        for t in range(0, CHUNK, 2):
            place = h * CHUNK + t
            row = jnp.where(place < HALO, place, jnp.maximum(n - 2 * HALO + place, 0))
            ap_pair(inner + place, row, a_all, 0, KA * cap, edge, edge_index)
        return 0

    lax.fori_loop(0, 2 * HALO // CHUNK, edge_rows, 0)
    aggregate(gmax - 1)

    def put_near(q, e, value):
        near[q, e] = value

    products(start_tab[0], start_tab[1], put_near)
    shift = jnp.clip(gmax - ga, 0, gmax - 1) + 1
    for o in range(BAND):
        lower = band[shift + 1, o]
        if o < WIDE:
            lower = lower + near[2, o]
        if o == 0:
            send[:, spill - 1] = pack(band[gmax - 1, BAND - 1], lower)
            continue
        upper = band[shift, o]
        if o <= WIDE:
            upper = upper + near[1, o - 1]
        send[:, fourth + o - 1] = pack(upper, lower)
    send_out(fourth, BAND - 1, 3)
    for o in range(BAND - 1):
        send[:, fifth + o] = pack(band[gmax - 1, o], band[gmax, o])
    for e in range(WIDE):
        send[:, spill + e] = pack(near[0, e], band[gmax + 1, e] + jnp.where(ga == 1, near[2, e], 0.0))
    send_out(fifth, BAND + WIDE, 4)

    def fill_row(c, carry):
        who, place = carry
        count = aggs[grp, who]
        slot = jnp.where(place < 2, gmax - 4 + place,
                         jnp.where(place >= count - 2, gmax + place - count, gmax - 2 + place - count))
        slot_tab[c] = jnp.clip(slot, 0, gmax - 1)
        who_tab[c] = who
        done = (place + 1 >= count).astype(jnp.int32)
        return jnp.minimum(who + done, members - 1), (1 - done) * (place + 1)

    lax.fori_loop(0, coarse, fill_row, (jnp.int32(0), jnp.int32(0)))

    def arrive(begin, size, index):
        lax.fori_loop(1, members, lambda s, _: (piece(s, begin, size, index).wait_recv(), 0)[1], 0)
        kept(begin, size, index).wait()

    def unpack(u, _):
        def body(who, _):
            for o in range(BAND):
                both = recv[who, u * BAND + o].astype(F32)
                band[2 * u, o, who] = both[:share]
                band[2 * u + 1, o, who] = both[share:]
            return 0

        return lax.fori_loop(0, members, body, 0)

    arrive(0, BAND, 0)
    unpack(0, 0)
    arrive(BAND, BAND, 1)
    unpack(1, 0)
    arrive(2 * BAND, fourth - 2 * BAND, 2)
    lax.fori_loop(2, pairs - 2, unpack, 0)
    nothing = jnp.zeros((share, tile), F32)
    arrive(fourth, BAND - 1, 3)

    def unpack_fourth(who, _):
        band[gmax - 4, 0, who] = nothing
        for o in range(1, BAND):
            both = recv[who, fourth + o - 1].astype(F32)
            band[gmax - 4, o, who] = both[:share]
            band[gmax - 3, o, who] = both[share:]
        return 0

    lax.fori_loop(0, members, unpack_fourth, 0)
    arrive(fifth, BAND + WIDE, 4)

    def unpack_fifth(who, _):
        for o in range(BAND - 1):
            both = recv[who, fifth + o].astype(F32)
            band[gmax - 2, o, who] = both[:share]
            band[gmax - 1, o, who] = both[share:]
        both = recv[who, spill - 1].astype(F32)
        band[gmax - 2, BAND - 1, who] = both[:share]
        band[gmax - 1, BAND - 1, who] = nothing
        band[gmax - 3, 0, who] = both[share:]
        return 0

    lax.fori_loop(0, members, unpack_fifth, 0)

    def unpack_spill(who, _):
        for e in range(WIDE):
            both = recv[who, spill + e].astype(F32)
            band[gmax, e + 2, who] = both[:share]
            band[gmax + 1, e, who] = both[share:]
        return 0

    lax.fori_loop(0, members, unpack_spill, 0)

    def add_spill(who, _):
        here, after = who, who + 1
        count = aggs[grp, who]
        for e in range(WIDE):
            band[gmax - 4, e, after] += band[gmax + 1, e, here]
            value = band[gmax, e + 2, after]
            band[gmax - 1, e + 2, here] += value
            band[gmax - 4, e + 2, here] += jnp.where(count == 1, value, 0.0)
            band[gmax - 3, e + 2, here] += jnp.where(count == 2, value, 0.0)
        return 0

    lax.fori_loop(0, members - 1, add_spill, 0)

    def coarse_row(row):
        row = jnp.clip(row, 0, coarse - 1)
        slot, who = slot_tab[row], who_tab[row]
        return [band[slot, o, who] for o in range(BAND)]

    def z_pack(way, base):
        def body(h, _):
            one, two = coarse_row(base + 2 * h), coarse_row(base + 2 * h + 1)
            for o in range(BAND):
                zsend[way, h * BAND + o] = jnp.concatenate([one[o], two[o]], axis=0).astype(BF16)
            return 0
        lax.fori_loop(0, (fmax + 1) // 2, body, 0)

    ways = [
        pltpu.make_async_remote_copy(
            src_ref=zsend.at[way], dst_ref=zrecv.at[way], send_sem=z_send.at[way], recv_sem=z_recv.at[way],
            device_id=(group, mem), device_id_type=MESH)
        for way, group in ((0, up), (1, down))
    ]
    z_pack(0, coarse - fmax)
    ways[0].start()
    z_pack(1, 0)
    ways[1].start()

    take_lower = flows[0, down]
    take_upper = flows[1, up]
    give_back = flows[1, grp]
    middle = coarse - flows[0, grp] - give_back
    foreign[2 * fmax + 2] = jnp.zeros((BAND, share, tile), F32)

    def place(slot):
        return jnp.where(slot < take_lower, slot - take_lower,
                         jnp.where(slot < take_lower + middle, give_back + slot - take_lower,
                                   coarse + slot - take_lower - middle))

    def in_middle(slot):
        for o, value in enumerate(coarse_row(place(slot))):
            outv[slot, o] = value

    def at_end(slot):
        row = place(slot)
        live = slot < take_lower + middle + take_upper
        native = jnp.logical_and(live, jnp.logical_and(row >= 0, row < coarse))
        index = jnp.where(live, jnp.where(row < 0, fmax + row, fmax + 1 + row - coarse), 2 * fmax + 2)
        other = foreign[jnp.clip(index, 0, 2 * fmax + 2)]
        for o, value in enumerate(coarse_row(row)):
            outv[slot, o] = jnp.where(native, value, other[o])

    def gather_all(fill, begin, end):
        def body(h, _):
            for t in range(4):
                fill(jnp.minimum(begin + 4 * h + t, end - 1))
            return 0
        lax.fori_loop(0, (end - begin + 3) // 4, body, 0)

    tail = 1 + coarse - 2 * fmax
    gather_all(in_middle, fmax, tail)

    def z_unpack(way, base):
        def body(h, _):
            for o in range(BAND):
                both = zrecv[way, h * BAND + o].astype(F32)
                foreign[base + 2 * h, o] = both[:share]
                foreign[base + 2 * h + 1, o] = both[share:]
            return 0
        lax.fori_loop(0, (fmax + 1) // 2, body, 0)

    for way in ways:
        way.wait_recv()
    z_unpack(0, 0)
    z_unpack(1, fmax + 1)
    for e in range(WIDE):
        foreign[fmax - 1, e + 2] += band[gmax, e + 2, 0]
        foreign[fmax + 1, e] += band[gmax + 1, e, members - 1]
    gather_all(at_end, 0, fmax)
    gather_all(at_end, tail, out_cap)
    for way in ways:
        way.wait_send()
    lax.fori_loop(1, members, lambda s, _: (piece(s, 0, total, 0).wait_send(), 0)[1], 0)
    for r in range(HALO):
        to_next(r).wait_send()
        to_prev(r).wait_send()


def local(a_tiles, p_tiles, a_offsets, agg_counts, row_counts, flows):
    cap, _, tile, _ = a_tiles.shape
    groups, members = lax.axis_size("grp"), lax.axis_size("mem")
    gmax = cap // 4
    pairs = gmax // 2
    coarse = members * gmax // 2
    fmax = coarse // 8
    share = tile // members
    pieces = pairs * BAND - 1 + WIDE
    out_cap = coarse + 2 * fmax - 2
    handed = (fmax + 1) // 2 * BAND
    smem = pl.BlockSpec(memory_space=pltpu.SMEM)
    hbm = pl.BlockSpec(memory_space=pl.ANY)
    vmem = pl.BlockSpec(memory_space=pltpu.VMEM)
    return pl.pallas_call(
        functools.partial(fused, (groups, members, cap, tile)),
        out_shape=pltpu.VMEM((out_cap, BAND, share, tile), F32),
        in_specs=[hbm, hbm, smem, smem, smem, smem],
        out_specs=vmem,
        scratch_shapes=[
            pltpu.VMEM((KA * EARLY + 1, tile, tile), BF16),
            pltpu.VMEM((KA * EARLY + 1, tile, tile), BF16),
            pltpu.VMEM((KA * cap + 1, tile, tile), BF16),
            pltpu.VMEM((STRIDE * cap + LEAD, tile, tile), BF16),
            pltpu.VMEM((STRIDE * 6 * HALO + LEAD, tile, tile), BF16),
            pltpu.VMEM((HALO * KP, tile, tile), BF16),
            pltpu.VMEM((cap, WIDE, tile, tile), BF16),
            pltpu.VMEM((cap + 1, KP * tile, tile), BF16),
            pltpu.VMEM((gmax + 2, BAND, members, share, tile), F32),
            pltpu.VMEM((KP, WIDE, members, share, tile), F32),
            pltpu.VMEM((members, pieces, 2 * share, tile), BF16),
            pltpu.VMEM((members, pieces, 2 * share, tile), BF16),
            pltpu.VMEM((2 * fmax + 3, BAND, share, tile), F32),
            pltpu.VMEM((2, handed, 2 * share, tile), BF16),
            pltpu.VMEM((2, handed, 2 * share, tile), BF16),
            pltpu.SMEM((gmax + 3,), jnp.int32),
            pltpu.SMEM((cap + 1,), jnp.int32),
            pltpu.SMEM((coarse,), jnp.int32),
            pltpu.SMEM((coarse,), jnp.int32),
            pltpu.SemaphoreType.DMA((3,)),
            pltpu.SemaphoreType.DMA,
            pltpu.SemaphoreType.DMA((2 * HALO,)),
            pltpu.SemaphoreType.DMA((2 * HALO,)),
            pltpu.SemaphoreType.DMA((members - 1,)),
            pltpu.SemaphoreType.DMA((5, members - 1)),
            pltpu.SemaphoreType.DMA((5,)),
            pltpu.SemaphoreType.DMA((2,)),
            pltpu.SemaphoreType.DMA((2,)),
        ],
        compiler_params=pltpu.CompilerParams(
            collective_id=0, has_side_effects=True, vmem_limit_bytes=58 * 1024 * 1024),
        cost_estimate=pl.CostEstimate(flops=7_500_000_000, bytes_accessed=20_000_000, transcendentals=0),
    )(a_tiles.reshape(cap * KA, tile, tile), p_tiles.reshape(cap * KP, tile, tile), a_offsets.T,
      agg_counts, row_counts, flows.T)


def solution(mesh):
    placed = (
        P(("grp", "mem"), None, None, None),
        P(("grp", "mem"), None, None, None),
        P(("grp", "mem"), None),
        P(),
        P(),
        P(),
    )
    return jax.shard_map(
        local, mesh=mesh, in_specs=placed, out_specs=P("grp", None, "mem", None), check_vma=False
    )
```
